512 devices in a mesh: tm: 32 (over x, y, z_hi), chan: 16 (over z_lo, core).
Axes of the slice: x: 4, y: 4, z: 16 (z_hi: 2, z_lo: 8; z = z_hi * 8 + z_lo), core: 2. Of those that a mesh axis runs over, the one named last changes fastest.
Arguments:
- waveform: bfloat16 [32768, 10240], P('tm', 'chan'), may hold values from -750 to 750
- templates: bfloat16 [16, 256, 10240], P(None, 'tm', 'chan'), may hold values from -40 to 40
Outputs:
- detection: float32 [16, 32768], P(None, ('tm', 'chan'))
The draws below stay inside these ranges and needn't reach their ends.
All inputs are finite; a program needn't handle non-finite values.
Results may differ from the reference program's by a relative error of at most 0.0003.
Values may be sent and summed in bfloat16 or wider, within the bound.
No kernel may reach another device: no remote copies, remote signals or barrier semaphores. Data moves between devices by JAX's collectives and lax.ppermute only.
A program may use at most 128 MiB of HBM per device.

```python
import math
import jax
import jax.numpy as jnp
from jax import lax

CH = 10240
L = 256
K = 16
SAMPLES = 32768


def draw_waveform(key, part):
    key = jax.random.fold_in(key, 11)
    first_key, second_key, third_key = jax.random.split(key, 3)
    ramp = jnp.exp(math.log(3.0) * jnp.arange(CH, dtype=jnp.float32) / (CH - 1))
    noise = jnp.clip(jax.random.normal(first_key, (SAMPLES, CH), jnp.float32), -6.0, 6.0)
    gains = ramp * jnp.exp(jax.random.uniform(second_key, (CH,), jnp.float32, 0.0, math.log(10.0)))
    envelope = jnp.exp(jax.random.uniform(third_key, (SAMPLES, 1), jnp.float32, math.log(0.3), math.log(3.0)))
    return (noise * gains[None, :] * envelope).astype(jnp.bfloat16)


def draw_templates(key, part):
    key = jax.random.fold_in(key, 23)
    first_key, second_key = jax.random.split(key, 2)
    ramp = jnp.exp(math.log(3.0) * jnp.arange(CH, dtype=jnp.float32) / (CH - 1))
    noise = jnp.clip(jax.random.normal(first_key, (K, L, CH), jnp.float32), -6.0, 6.0)
    gains = jnp.exp(jax.random.uniform(second_key, (K, 1, CH), jnp.float32, math.log(0.5), math.log(2.0)))
    return (noise * gains * ramp[None, None, :]).astype(jnp.bfloat16)


def setup_inputs(seed: int = 0) -> dict:
    seeds = jax.random.split(jax.random.key(seed), 3)
    return {
        "waveform": draw_waveform(jax.random.fold_in(seeds[2], 71), 0),
        "templates": draw_templates(jax.random.fold_in(seeds[2], 71), 0),
    }


def reference(waveform, templates):
    sample_rows = waveform.shape[0]
    padded = jnp.concatenate([waveform, jnp.zeros((L - 1, waveform.shape[1]), waveform.dtype)], axis=0)
    padded_rows = sample_rows + L - 1
    group_size = math.gcd(L, 32)

    def one_group(group_index, running):
        lag_block = lax.dynamic_slice_in_dim(templates, group_index * group_size, group_size, 1)
        flat_block = lag_block.reshape(K * group_size, lag_block.shape[2])
        products = lax.dot_general(flat_block, padded, (((1,), (1,)), ((), ())), preferred_element_type=jnp.float32)
        products = products.reshape(K, group_size * padded_rows)
        products = jnp.pad(products, ((0, 0), (0, group_size)))
        products = products.reshape(K, group_size, padded_rows + 1)
        window = lax.dynamic_slice_in_dim(products, group_index * group_size, sample_rows, 2)
        return running + lax.optimization_barrier(jnp.sum(window, axis=1))
    stack = lax.fori_loop(0, L // group_size, one_group, jnp.zeros((K, sample_rows), jnp.float32))
    squares = lax.optimization_barrier(jnp.sum(jnp.square(padded.astype(jnp.float32)), axis=1))
    data_energy = lax.reduce_window(squares, jnp.float32(0.0), lax.add, (L,), (1,), 'VALID')
    tpl_values = templates.astype(jnp.float32)
    template_energy = lax.optimization_barrier(jnp.sum(tpl_values * tpl_values, axis=(1, 2)))
    norm_scale = math.sqrt(L * CH)
    return stack * norm_scale * lax.rsqrt(data_energy + 1e-06)[None, :] * lax.rsqrt(template_energy)[:, None]
```

```python
import math

import jax
import jax.numpy as jnp
from jax import lax
from jax.experimental import pallas as pl
from jax.experimental.pallas import tpu as pltpu
from jax.sharding import PartitionSpec as P

CH = 10240
L = 256
K = 16
SUB = 8
ROWS = 1024
RIM = 256
SPAN = ROWS + 128
NT = (((1,), (1,)), ((), ()))


def correlate_kernel(z_ref, x_ref, rim_ref, own_ref, oth_ref, out_ref, xs, q):
    xs[0:ROWS] = x_ref[...]
    xs[ROWS : ROWS + RIM] = rim_ref[...]
    used = ROWS + 16

    def step(i, te):
        w = jnp.concatenate([own_ref[i], oth_ref[i]], axis=0)
        rows = pl.ds(pl.multiple_of(16 * i, 16), used)
        part = lax.dot_general(xs[rows, :], w, NT, preferred_element_type=jnp.float32)
        q[0:used, :] = jnp.where(i == 0, part, q[0:used, :] + part)
        wf = w.astype(jnp.float32)
        sq = wf * wf
        for j in range(5):
            te = te + sq[:, 128 * j : 128 * j + 128]
        return te

    te = lax.fori_loop(0, 16, step, jnp.zeros((2 * K * SUB, 128), jnp.float32))
    te = jnp.sum(te.reshape(2, K, SUB, 128), axis=(0, 2))
    te = jnp.sum(te, axis=1, keepdims=True)

    q[used:SPAN, :] = jnp.zeros((SPAN - used, 2 * K * SUB), jnp.float32)
    halves = []
    for h in range(2):
        p = jnp.transpose(q[:, 128 * h : 128 * h + 128])
        p = p.reshape(K, SUB, SPAN)
        lag = lax.broadcasted_iota(jnp.int32, (K, SUB, SPAN), 1)
        for b in (1, 2, 4):
            p = jnp.where((lag & b) != 0, pltpu.roll(p, SPAN - b, 2), p)
        halves.append(jnp.sum(p, axis=1))
    shift = [pltpu.roll(p, SPAN - SUB, 1) for p in halves]
    upper = z_ref[0] == 1
    stack = jnp.where(upper, shift[0] + halves[1], halves[0] + shift[1])

    sq = jnp.zeros((ROWS + RIM, 128), jnp.float32)
    for j in range(5):
        v = xs[:, 128 * j : 128 * j + 128].astype(jnp.float32)
        sq = sq + v * v
    de = jnp.sum(jnp.transpose(sq), axis=0, keepdims=True)
    de = jnp.broadcast_to(de, (8, ROWS + RIM))
    for b in range(8):
        de = de + pltpu.roll(de, ROWS + RIM - (1 << b), 1)

    lane = lax.broadcasted_iota(jnp.int32, (8, 128), 1)
    te_row = jnp.where(lane < 96, te[0:8], te[8:16])
    for d in range(16):
        tile = slice(128 * (d // 2), 128 * (d // 2) + 128)
        lo, hi, en = stack[0:8, tile], stack[8:16, tile], de[:, tile]
        if d % 2 == 0:
            hi = pltpu.roll(hi, 64, 1)
        else:
            lo, en = pltpu.roll(lo, 64, 1), pltpu.roll(en, 64, 1)
        out_ref[d, 0:8, :] = jnp.where(lane < 64, lo, hi)
        out_ref[d, 8:16, :] = jnp.where(lane < 64, en, te_row)


def correlate(z, x, rim, own, oth):
    vmem = pl.BlockSpec(memory_space=pltpu.VMEM)
    return pl.pallas_call(
        correlate_kernel,
        out_shape=jax.ShapeDtypeStruct((16, 16, 128), jnp.float32),
        in_specs=[pl.BlockSpec(memory_space=pltpu.SMEM), vmem, vmem, vmem, vmem],
        out_specs=vmem,
        scratch_shapes=[
            pltpu.VMEM((ROWS + RIM, 640), jnp.bfloat16),
            pltpu.VMEM((SPAN, 2 * K * SUB), jnp.float32),
        ],
        compiler_params=pltpu.CompilerParams(vmem_limit_bytes=40 * 2**20),
        cost_estimate=pl.CostEstimate(flops=5_500_000_000, bytes_accessed=7_000_000, transcendentals=0),
        name="correlate",
    )(z, x, rim, own, oth)


def finish_kernel(parts_ref, out_ref):
    total = jnp.sum(parts_ref[...], axis=0)
    scale = math.sqrt(L * CH)
    rows, energies = total[0:8], total[8:16]
    inv = lax.rsqrt(energies[:, 0:64] + 1e-06) * scale
    out_ref[0:8, :] = rows[:, 0:64] * inv * lax.rsqrt(energies[:, 64:65])
    out_ref[8:16, :] = rows[:, 64:128] * inv * lax.rsqrt(energies[:, 96:97])


def finish(parts):
    vmem = pl.BlockSpec(memory_space=pltpu.VMEM)
    return pl.pallas_call(
        finish_kernel,
        out_shape=jax.ShapeDtypeStruct((K, 64), jnp.float32),
        in_specs=[vmem],
        out_specs=vmem,
        name="finish",
    )(parts)


def local(waveform, templates):
    tm = lax.axis_size("tm")
    z = lax.rem(lax.axis_index("tm"), 2)
    plane = [[2 * i + h for i in range(tm // 2)] for h in range(2)]
    shard = templates.reshape(K * SUB, -1)
    other = lax.ppermute(shard, "tm", [(i, i ^ 1) for i in range(tm)])
    rim = lax.ppermute(waveform[:RIM], "tm", [(i, i - 1) for i in range(1, tm)])

    def spread(block):
        copies = jnp.broadcast_to(block[None], (tm // 2,) + block.shape)
        return lax.all_to_all(copies, "tm", 0, 0, axis_index_groups=plane)

    own_all = spread(shard)
    oth_all = spread(other)
    parts = correlate(z.reshape(1), waveform, rim, own_all, oth_all)
    parts = lax.all_to_all(parts, "chan", 0, 0)
    return finish(parts)


def solution(mesh):
    in_specs = (P("tm", "chan"), P(None, "tm", "chan"))
    out_specs = P(None, ("tm", "chan"))
    return jax.shard_map(local, mesh=mesh, in_specs=in_specs, out_specs=out_specs, check_vma=False)
```

```python
import math

import jax
import jax.numpy as jnp
from jax import lax
from jax.experimental import pallas as pl
from jax.experimental.pallas import tpu as pltpu
from jax.sharding import PartitionSpec as P

CH = 10240
L = 256
K = 16
SUB = 8
ROWS = 1024
RIM = 256
USED = ROWS + 16
SPAN = ROWS + 128
NN = (((1,), (0,)), ((), ()))


def swap(v):
    return jnp.concatenate([v[:, 64:], v[:, :64]], axis=1)


def low_lanes():
    return lax.broadcasted_iota(jnp.int32, (1, 128), 1) < 64


def pack_rest(v, half):
    n = v.shape[0] // 2
    if half == 0:
        return jnp.where(low_lanes(), v[:n], swap(v[n:]))
    return jnp.where(low_lanes(), swap(v[:n]), v[n:])


def pack_rows(src, n, half, keep_ref, send_ref, blank=None):
    rest = src[:, 512:640]
    first, second = pack_rest(rest, 0), pack_rest(rest, 1)
    one = half == 1
    for ref, other in ((keep_ref, False), (send_ref, True)):
        upper = jnp.logical_not(one) if other else one
        parts = [
            jnp.where(upper, src[:, 256:384], src[:, 0:128]),
            jnp.where(upper, src[:, 384:512], src[:, 128:256]),
            jnp.where(upper, second, first),
        ]
        at = 0
        for part in parts:
            if blank is not None:
                part = jnp.where(blank, jnp.zeros_like(part), part)
            ref[at : at + part.shape[0]] = part
            at += part.shape[0]


def pack_lags(src, copies_ref):
    rest = src[:, 512:640]
    for half in range(2):
        packed = jnp.concatenate(
            [src[:, 256 * half : 256 * half + 128], src[:, 256 * half + 128 : 256 * half + 256], pack_rest(rest, half)],
            axis=0,
        )
        for p in range(16):
            if (p // 4) % 2 == half:
                copies_ref[p] = packed


def first_pack_kernel(place_ref, x_ref, t_ref, keep_ref, send_ref, copies_ref):
    pack_rows(x_ref[...], ROWS, place_ref[1], keep_ref, send_ref)
    pack_lags(t_ref[...], copies_ref)


def second_pack_kernel(place_ref, c_ref, keep_ref, send_ref, copies_ref):
    pack_lags(c_ref[0:128], copies_ref)
    pack_rows(c_ref[128:384], RIM, place_ref[1], keep_ref, send_ref, blank=place_ref[2] == 1)


VMEM = pl.BlockSpec(memory_space=pltpu.VMEM)
SMEM = pl.BlockSpec(memory_space=pltpu.SMEM)


def packed(kernel, rows, name, *args):
    half = jax.ShapeDtypeStruct((rows * 5 // 2, 128), jnp.bfloat16)
    return pl.pallas_call(
        kernel,
        out_shape=(half, half, jax.ShapeDtypeStruct((16, 320, 128), jnp.bfloat16)),
        in_specs=[SMEM] + [VMEM] * (len(args) - 1),
        out_specs=(VMEM, VMEM, VMEM),
        compiler_params=pltpu.CompilerParams(vmem_limit_bytes=32 * 2**20),
        cost_estimate=pl.CostEstimate(flops=2_000_000, bytes_accessed=4_000_000, transcendentals=0),
        name=name,
    )(*args)


def lay_out(xm, x2, b, body, rim):
    for c in range(2):
        lanes = slice(128 * c, 128 * c + 128)
        xm[b, 0:ROWS, lanes] = body[ROWS * c : ROWS * c + ROWS]
        xm[b, ROWS : ROWS + RIM, lanes] = rim[RIM * c : RIM * c + RIM]
    p, r = body[2 * ROWS :], rim[2 * RIM :]
    left = jnp.concatenate([p, swap(p), r, swap(r)], axis=0)
    right = jnp.concatenate([swap(p), p, swap(r), r], axis=0)
    n = ROWS + RIM
    x2[b, 0 : n - 16] = jnp.where(low_lanes(), left[0 : n - 16], right[16:n])
    x2[b, n - 16 : n] = jnp.where(low_lanes(), left[n - 16 : n], jnp.zeros((16, 128), left.dtype))


def lag_pair(ref, even, odd):
    pe, po = ref[even, 256:320], ref[odd, 256:320]
    rest = jnp.concatenate(
        [jnp.where(low_lanes(), pe, swap(po)), jnp.where(low_lanes(), swap(pe), po)], axis=0
    )
    return jnp.concatenate(
        [ref[even, 0:128], ref[even, 128:256], ref[odd, 0:128], ref[odd, 128:256], rest], axis=1
    )


def correlate_kernel(place_ref, keep_ref, got_ref, rimk_ref, rimg_ref, own_ref, oth_ref, out_ref, xm, x2, q):
    z, half = place_ref[0], place_ref[1]
    lay_out(xm, x2, 0, keep_ref, rimk_ref)
    lay_out(xm, x2, 1, got_ref, rimg_ref)

    te = jnp.zeros((2 * K * SUB, 128), jnp.float32)
    for s in range(2):
        ws = []
        for a in range(4 * s, 4 * s + 4):
            even = lax.rem(2 * a + 15 * z, 16)
            odd = lax.rem(2 * a + 1 + 15 * z, 16)
            w = jnp.concatenate([lag_pair(own_ref, 2 * a, 2 * a + 1), lag_pair(oth_ref, even, odd)], axis=0)
            wf = w.astype(jnp.float32)
            sq = wf * wf
            for j in range(5):
                te = te + sq[:, 128 * j : 128 * j + 128]
                ws.append(jnp.transpose(w[:, 128 * j : 128 * j + 128]))
        w = jnp.concatenate(ws, axis=0)
        for b in range(2):
            rows = []
            for a in range(4 * s, 4 * s + 4):
                r = 32 * a
                rows += [xm[b, r : r + USED], xm[b, r + 16 : r + 16 + USED], x2[b, r : r + USED]]
            part = lax.dot_general(jnp.concatenate(rows, axis=1), w, NN, preferred_element_type=jnp.float32)
            q[b, 0:USED, :] = part if s == 0 else q[b, 0:USED, :] + part
    te = jnp.sum(te.reshape(2, K, SUB, 128), axis=(0, 2))
    te = jnp.sum(te, axis=1, keepdims=True)

    lane = lax.broadcasted_iota(jnp.int32, (8, 128), 1)
    te_row = jnp.where(lane < 96, te[0:8], te[8:16])
    for b in range(2):
        q[b, USED:SPAN, :] = jnp.zeros((SPAN - USED, 2 * K * SUB), jnp.float32)
        sums = []
        for g in range(2):
            p = jnp.transpose(q[b, :, 128 * g : 128 * g + 128])
            p = p.reshape(K, SUB, SPAN)
            p = pltpu.roll(p, SPAN - (SUB - 1), 2, stride=1, stride_axis=1)
            sums.append(jnp.sum(p, axis=1))
        late = [pltpu.roll(p, SPAN - SUB, 1) for p in sums]
        stack = jnp.where(z == 1, late[0] + sums[1], sums[0] + late[1])

        sq = jnp.zeros((ROWS + RIM, 128), jnp.float32)
        for v in (xm[b, :, 0:128], xm[b, :, 128:256], jnp.where(low_lanes(), x2[b], jnp.zeros_like(x2[b]))):
            v = v.astype(jnp.float32)
            sq = sq + v * v
        de = jnp.sum(jnp.transpose(sq), axis=0, keepdims=True)
        de = jnp.broadcast_to(de, (8, ROWS + RIM))
        for i in range(8):
            de = de + pltpu.roll(de, ROWS + RIM - (1 << i), 1)

        at = 16 * jnp.where(half == b, 0, 1)
        for d in range(16):
            tile = slice(128 * (d // 2), 128 * (d // 2) + 128)
            lo, hi, en = stack[0:8, tile], stack[8:16, tile], de[:, tile]
            if d % 2 == 0:
                hi = pltpu.roll(hi, 64, 1)
            else:
                lo, en = pltpu.roll(lo, 64, 1), pltpu.roll(en, 64, 1)
            out_ref[at + d, 0:8, :] = jnp.where(lane < 64, lo, hi)
            out_ref[at + d, 8:16, :] = jnp.where(lane < 64, en, te_row)


def correlate(*args):
    return pl.pallas_call(
        correlate_kernel,
        out_shape=jax.ShapeDtypeStruct((32, 16, 128), jnp.float32),
        in_specs=[SMEM] + [VMEM] * 6,
        out_specs=VMEM,
        scratch_shapes=[
            pltpu.VMEM((2, ROWS + RIM, 256), jnp.bfloat16),
            pltpu.VMEM((2, ROWS + RIM, 128), jnp.bfloat16),
            pltpu.VMEM((2, SPAN, 2 * K * SUB), jnp.float32),
        ],
        compiler_params=pltpu.CompilerParams(vmem_limit_bytes=48 * 2**20),
        cost_estimate=pl.CostEstimate(flops=5_500_000_000, bytes_accessed=5_000_000, transcendentals=0),
        name="correlate",
    )(*args)


def finish_kernel(parts_ref, out_ref):
    total = jnp.sum(parts_ref[...], axis=0)
    scale = math.sqrt(L * CH)
    rows, energies = total[0:8], total[8:16]
    inv = lax.rsqrt(energies[:, 0:64] + 1e-06) * scale
    out_ref[0:8, :] = rows[:, 0:64] * inv * lax.rsqrt(energies[:, 64:65])
    out_ref[8:16, :] = rows[:, 64:128] * inv * lax.rsqrt(energies[:, 96:97])


def finish(parts):
    return pl.pallas_call(
        finish_kernel,
        out_shape=jax.ShapeDtypeStruct((K, 64), jnp.float32),
        in_specs=[VMEM],
        out_specs=VMEM,
        name="finish",
    )(parts)


def local(waveform, templates):
    tm = lax.axis_size("tm")
    chan = lax.axis_size("chan")
    me = lax.axis_index("tm")
    half = lax.rem(me // 8, 2)
    place = jnp.stack([lax.rem(me, 2), half, (me == tm - 1).astype(jnp.int32)])
    plane = [[2 * i + h for i in range(tm // 2)] for h in range(2)]
    partner = [(i, i ^ 8) for i in range(tm)]

    shard = jnp.flip(templates, 1).reshape(K * SUB, -1)
    ahead = jnp.concatenate([shard, waveform[:RIM]], axis=0)
    ahead = lax.ppermute(ahead, "tm", [(i, (i - 1) % tm) for i in range(tm)])

    keep, send, copies = packed(first_pack_kernel, ROWS, "first_pack", place, waveform, shard)
    got = lax.ppermute(send, "tm", partner)
    own = lax.all_to_all(copies, "tm", 0, 0, axis_index_groups=plane)

    rim_keep, rim_send, copies = packed(second_pack_kernel, RIM, "second_pack", place, ahead)
    rim_got = lax.ppermute(rim_send, "tm", partner)
    oth = lax.all_to_all(copies, "tm", 0, 0, axis_index_groups=plane)

    parts = correlate(place, keep, got, rim_keep, rim_got, own, oth)
    pairs = [
        [t * chan + c for t in (i, i ^ 8) for c in range(chan)] for i in range(tm) if i & 8 == 0
    ]
    parts = lax.all_to_all(parts, ("tm", "chan"), 0, 0, axis_index_groups=pairs)
    return finish(parts)


def solution(mesh):
    in_specs = (P("tm", "chan"), P(None, "tm", "chan"))
    out_specs = P(None, ("tm", "chan"))
    return jax.shard_map(local, mesh=mesh, in_specs=in_specs, out_specs=out_specs, check_vma=False)
```

```python
import math

import jax
import jax.numpy as jnp
from jax import lax
from jax.experimental import pallas as pl
from jax.experimental.pallas import tpu as pltpu
from jax.sharding import PartitionSpec as P

CH = 10240
L = 256
K = 16
SUB = 8
ROWS = 1024
RIM = 256
USED = ROWS + 16
SPAN = ROWS + 128
EDGE_USED = RIM + 16
EDGE_SPAN = RIM + 128
NN = (((1,), (0,)), ((), ()))
BF16 = jnp.bfloat16
VMEM = pl.BlockSpec(memory_space=pltpu.VMEM)
SMEM = pl.BlockSpec(memory_space=pltpu.SMEM)
ANY = pl.BlockSpec(memory_space=pl.ANY)


def swap(v):
    return jnp.concatenate([v[:, 64:], v[:, :64]], axis=1)


def low_lanes():
    return lax.broadcasted_iota(jnp.int32, (1, 128), 1) < 64


def pack_rest(v, half):
    n = v.shape[0] // 2
    if half == 0:
        return jnp.where(low_lanes(), v[:n], swap(v[n:]))
    return jnp.where(low_lanes(), swap(v[:n]), v[n:])


def pack_half(v, half, upper):
    return [
        jnp.where(upper, v[:, 256:384], v[:, 0:128]),
        jnp.where(upper, v[:, 384:512], v[:, 128:256]),
        jnp.where(upper, pack_rest(v[:, 512:640], 1), pack_rest(v[:, 512:640], 0)),
    ]


def first_pack_kernel(place, x, send):
    at = 0
    for part in pack_half(x[...], None, place[1] == 0):
        send[at : at + part.shape[0]] = part
        at += part.shape[0]


def lag_pack_kernel(lags, copies, packed, sems):
    i = lax.broadcasted_iota(jnp.int32, (K * SUB, K * SUB), 0)
    j = lax.broadcasted_iota(jnp.int32, (K * SUB, K * SUB), 1)
    order = (i // SUB * SUB + (SUB - 1 - i % SUB) == j).astype(BF16)
    v = lax.dot_general(order, lags[...], NN, preferred_element_type=jnp.float32).astype(BF16)
    for half in range(2):
        packed[half, 0:128] = v[:, 256 * half : 256 * half + 128]
        packed[half, 128:256] = v[:, 256 * half + 128 : 256 * half + 256]
        packed[half, 256:320] = pack_rest(v[:, 512:640], half)
    moves = [pltpu.make_async_copy(packed.at[p // 8], copies.at[p], sems.at[p]) for p in range(16)]
    for move in moves:
        move.start()
    for move in moves:
        move.wait()


def first_pack(place, x):
    return pl.pallas_call(
        first_pack_kernel,
        out_shape=jax.ShapeDtypeStruct((ROWS * 5 // 2, 128), BF16),
        in_specs=[SMEM, VMEM],
        out_specs=VMEM,
        compiler_params=pltpu.CompilerParams(vmem_limit_bytes=16 * 2**20),
        cost_estimate=pl.CostEstimate(flops=2_000_000, bytes_accessed=2_000_000, transcendentals=0),
        name="first_pack",
    )(place, x)


def lag_pack(lags):
    return pl.pallas_call(
        lag_pack_kernel,
        out_shape=jax.ShapeDtypeStruct((16, 320, 128), BF16),
        in_specs=[VMEM],
        out_specs=ANY,
        scratch_shapes=[pltpu.VMEM((2, 320, 128), BF16), pltpu.SemaphoreType.DMA((16,))],
        cost_estimate=pl.CostEstimate(flops=2_000_000, bytes_accessed=1_500_000, transcendentals=0),
        name="lag_pack",
    )(lags)


def lanes_of(half, c):
    return pl.ds(pl.multiple_of(256 * half + 128 * c, 128), 128)


def lag_pair(ref, even, odd):
    pe, po = ref[even, 256:320], ref[odd, 256:320]
    rest = jnp.concatenate(
        [jnp.where(low_lanes(), pe, swap(po)), jnp.where(low_lanes(), swap(pe), po)], axis=0
    )
    return jnp.concatenate(
        [ref[even, 0:128], ref[even, 128:256], ref[odd, 0:128], ref[odd, 128:256], rest], axis=1
    )


def sum_lags(xm, x2, q, own, oth, used, with_energy):
    te = jnp.zeros((2 * K * SUB, 128), jnp.float32)
    for s in range(2):
        ws = []
        for a in range(4 * s, 4 * s + 4):
            w = jnp.concatenate([lag_pair(ref, 2 * a, 2 * a + 1) for ref in (own, oth)], axis=0)
            if with_energy:
                wf = w.astype(jnp.float32)
                sq = wf * wf
                for j in range(5):
                    te = te + sq[:, 128 * j : 128 * j + 128]
            for j in range(5):
                ws.append(jnp.transpose(w[:, 128 * j : 128 * j + 128]))
        w = jnp.concatenate(ws, axis=0)
        for b in range(2):
            rows = []
            for a in range(4 * s, 4 * s + 4):
                r = 32 * a
                rows += [xm[b, r : r + used], xm[b, r + 16 : r + 16 + used], x2[b, r : r + used]]
            part = lax.dot_general(jnp.concatenate(rows, axis=1), w, NN, preferred_element_type=jnp.float32)
            q[b, 0:used, :] = part if s == 0 else q[b, 0:used, :] + part
    te = jnp.sum(te.reshape(2, K, SUB, 128), axis=(0, 2))
    te = jnp.sum(te, axis=1, keepdims=True)
    lane = lax.broadcasted_iota(jnp.int32, (K, 128), 1)
    row = lax.broadcasted_iota(jnp.int32, (K, 128), 0)
    return jnp.sum(jnp.where(lane == 64 + row, te, 0.0), axis=0, keepdims=True)


def sum_fine_lags(q, b, span, used, z):
    q[b, used:span, :] = jnp.zeros((span - used, 2 * K * SUB), jnp.float32)
    sums = []
    for g in range(2):
        p = jnp.transpose(q[b, :, 128 * g : 128 * g + 128])
        p = p.reshape(K, SUB, span)
        p = pltpu.roll(p, span - (SUB - 1), 2, stride=1, stride_axis=1)
        sums.append(jnp.sum(p, axis=1))
    late = [pltpu.roll(p, span - SUB, 1) for p in sums]
    return jnp.where(z == 1, late[0] + sums[1], sums[0] + late[1])


def window_energy(xm, x2, b, n):
    sq = jnp.zeros((n, 128), jnp.float32)
    rest = x2[b, 0:n]
    for v in (xm[b, 0:n, 0:128], xm[b, 0:n, 128:256], jnp.where(low_lanes(), rest, jnp.zeros_like(rest))):
        v = v.astype(jnp.float32)
        sq = sq + v * v
    de = jnp.sum(jnp.transpose(sq), axis=0, keepdims=True)
    de = jnp.broadcast_to(de, (8, n))
    for i in range(8):
        de = de + pltpu.roll(de, n - (1 << i), 1)
    return de


def store(out, at, stack, de, te_row, count):
    low = low_lanes()
    for d in range(count):
        tile = slice(128 * (d // 2), 128 * (d // 2) + 128)
        lo, hi, en = stack[0:8, tile], stack[8:16, tile], de[:, tile]
        if d % 2 == 0:
            hi = pltpu.roll(hi, 64, 1)
        else:
            lo, en = pltpu.roll(lo, 64, 1), pltpu.roll(en, 64, 1)
        both = jnp.where(low, lo, hi)
        for r in range(8):
            out[at + d, :, 128 * r : 128 * r + 128] = both[r : r + 1]
        out[at + d, :, 1024:1152] = jnp.where(low, en[0:1], te_row)


def lay_out_rest(x2, b, left, right, before, after):
    zeros = [jnp.zeros((n, 128), BF16) for n in (before, after)]
    left = jnp.concatenate([v for v in (zeros[0], left, zeros[1]) if v.shape[0]], axis=0)
    right = jnp.concatenate([v for v in (zeros[0], right, zeros[1]) if v.shape[0]], axis=0)
    n = left.shape[0]
    x2[b, 0 : n - 16] = jnp.where(low_lanes(), left[0 : n - 16], right[16:n])
    x2[b, n - 16 : n] = jnp.where(low_lanes(), left[n - 16 : n], jnp.zeros((16, 128), BF16))


def fetch(x, got, own, oth, half, rows, at, xm, mine, his, lo_lags, hi_lags, sems):
    first = [
        pltpu.make_async_copy(x.at[pl.ds(0, rows), pl.ds(512, 128)], mine, sems.at[0]),
        pltpu.make_async_copy(got.at[pl.ds(2 * ROWS, his.shape[0])], his, sems.at[1]),
    ]
    second = [
        pltpu.make_async_copy(own, lo_lags, sems.at[2]),
        pltpu.make_async_copy(oth, hi_lags, sems.at[3]),
    ]
    for c in range(2):
        lanes, body = pl.ds(128 * c, 128), pl.ds(at, rows)
        second += [
            pltpu.make_async_copy(x.at[pl.ds(0, rows), lanes_of(half, c)], xm.at[0, body, lanes], sems.at[4 + c]),
            pltpu.make_async_copy(got.at[pl.ds(ROWS * c, rows)], xm.at[1, body, lanes], sems.at[6 + c]),
        ]
    for move in first + second:
        move.start()
    return first, second


def edge_kernel(place, x, got, own, oth, edges, xm, x2, q, mine, his, lo_lags, hi_lags, sums, sems):
    z, half = place[0], place[1]
    first, second = fetch(x, got, own, oth, half, RIM, RIM, xm, mine, his, lo_lags, hi_lags, sems)
    for move in first:
        move.wait()
    for b in range(2):
        xm[b, 0:RIM] = jnp.zeros((RIM, 256), BF16)
        if b == 0:
            v = mine[...]
            left, right = jnp.where(half == 1, swap(v), v), jnp.where(half == 1, v, swap(v))
        else:
            p = his[...]
            left, right = p, swap(p)
        lay_out_rest(x2, b, left, right, RIM, 0)
    for move in second:
        move.wait()
    sum_lags(xm, x2, q, lo_lags, hi_lags, EDGE_USED, False)
    for b in range(2):
        stack = sum_fine_lags(q, b, EDGE_SPAN, EDGE_USED, z)
        de = window_energy(xm, x2, b, 2 * RIM)
        store(sums, 4 * b, stack, de, jnp.zeros((1, 128), jnp.float32), 4)
    low = jnp.where(half == 1, sums[4:8], sums[0:4])
    high = jnp.where(half == 1, sums[0:4], sums[4:8])
    turn = place[2] == 1
    edges[0:4] = jnp.where(turn, high, low)
    edges[4:8] = jnp.where(turn, jnp.zeros_like(high), high)


def main_kernel(place, x, got, own, oth, out, xm, x2, q, mine, his, lo_lags, hi_lags, sems):
    z, half = place[0], place[1]
    first, second = fetch(x, got, own, oth, half, ROWS, 0, xm, mine, his, lo_lags, hi_lags, sems)
    for move in first:
        move.wait()
    for b in range(2):
        xm[b, ROWS:] = jnp.zeros((RIM, 256), BF16)
        if b == 0:
            v = mine[...]
            left, right = jnp.where(half == 1, swap(v), v), jnp.where(half == 1, v, swap(v))
        else:
            p = his[...]
            left, right = jnp.concatenate([p, swap(p)], axis=0), jnp.concatenate([swap(p), p], axis=0)
        lay_out_rest(x2, b, left, right, 0, RIM)
    for move in second:
        move.wait()
    te_row = sum_lags(xm, x2, q, lo_lags, hi_lags, USED, True)
    for b in range(2):
        stack = sum_fine_lags(q, b, SPAN, USED, z)
        de = window_energy(xm, x2, b, ROWS + RIM)
        store(out, 16 * jnp.where(half == b, 0, 1), stack, de, te_row, 16)


def scratch(rows, span, his_rows):
    return [
        pltpu.VMEM((2, rows + RIM, 256), BF16),
        pltpu.VMEM((2, rows + RIM, 128), BF16),
        pltpu.VMEM((2, span, 2 * K * SUB), jnp.float32),
        pltpu.VMEM((rows, 128), BF16),
        pltpu.VMEM((his_rows, 128), BF16),
        pltpu.VMEM((16, 320, 128), BF16),
        pltpu.VMEM((16, 320, 128), BF16),
    ]


def edge_sums(*args):
    return pl.pallas_call(
        edge_kernel,
        out_shape=jax.ShapeDtypeStruct((8, 1, 1152), jnp.float32),
        in_specs=[SMEM] + [ANY] * 4,
        out_specs=VMEM,
        scratch_shapes=scratch(RIM, EDGE_SPAN, RIM)
        + [pltpu.VMEM((8, 1, 1152), jnp.float32), pltpu.SemaphoreType.DMA((8,))],
        compiler_params=pltpu.CompilerParams(vmem_limit_bytes=32 * 2**20),
        cost_estimate=pl.CostEstimate(flops=1_400_000_000, bytes_accessed=3_200_000, transcendentals=0),
        name="edge_sums",
    )(*args)


def main_sums(*args):
    return pl.pallas_call(
        main_kernel,
        out_shape=jax.ShapeDtypeStruct((32, 1, 1152), jnp.float32),
        in_specs=[SMEM] + [ANY] * 4,
        out_specs=VMEM,
        scratch_shapes=scratch(ROWS, SPAN, ROWS // 2) + [pltpu.SemaphoreType.DMA((8,))],
        compiler_params=pltpu.CompilerParams(vmem_limit_bytes=48 * 2**20),
        cost_estimate=pl.CostEstimate(flops=5_500_000_000, bytes_accessed=5_000_000, transcendentals=0),
        name="main_sums",
    )(*args)


def finish_kernel(parts, out):
    total = jnp.sum(parts[...], axis=0)
    scale = math.sqrt(L * CH)
    rows = jnp.concatenate([total[:, 128 * r : 128 * r + 128] for r in range(8)], axis=0)
    last = total[:, 1024:1152]
    lane = lax.broadcasted_iota(jnp.int32, (K, 128), 1)
    row = lax.broadcasted_iota(jnp.int32, (K, 128), 0)
    te = jnp.sum(jnp.where(lane == 64 + row, last, 0.0), axis=1, keepdims=True)
    both = jnp.concatenate([rows[:, 0:64], rows[:, 64:128]], axis=0)
    out[...] = both * scale * lax.rsqrt(last[:, 0:64] + 1e-06) * lax.rsqrt(te)


def finish(parts):
    return pl.pallas_call(
        finish_kernel,
        out_shape=jax.ShapeDtypeStruct((K, 64), jnp.float32),
        in_specs=[VMEM],
        out_specs=VMEM,
        name="finish",
    )(parts)


def local(waveform, templates):
    tm = lax.axis_size("tm")
    chan = lax.axis_size("chan")
    me = lax.axis_index("tm")
    half = me // 16
    turn = jnp.logical_and(lax.rem(me, 8) == 0, lax.rem(me // 8, 2) == 0)
    place = jnp.stack([lax.rem(me, 2), half, turn.astype(jnp.int32)])
    plane = [[2 * i + h for i in range(tm // 2)] for h in range(2)]
    partner = [(i, i ^ 16) for i in range(tm)]

    shard = templates.reshape(K * SUB, -1)
    other = lax.ppermute(shard, "tm", [(i, i ^ 1) for i in range(tm)])
    got = lax.ppermute(first_pack(place, waveform), "tm", partner)

    def spread(lags):
        return lax.all_to_all(lag_pack(lags), "tm", 0, 0, axis_index_groups=plane)

    own = spread(shard)
    other, got = lax.optimization_barrier((other, got))
    oth = spread(other)

    edges = edge_sums(place, waveform, got, own, oth)
    edges = lax.ppermute(edges, "tm", [(i, i - 1 if i % 8 else (i ^ 8) + 7) for i in range(tm)])

    parts = main_sums(place, waveform, got, own, oth)
    edges = jnp.pad(edges.reshape(2, 4, 1, 1152), ((0, 0), (12, 0), (0, 0), (0, 0)))
    parts = parts + edges.reshape(parts.shape)
    pairs = [[t * chan + c for t in (i, i ^ 16) for c in range(chan)] for i in range(tm // 2)]
    parts = lax.all_to_all(parts, ("tm", "chan"), 0, 0, axis_index_groups=pairs)
    return finish(parts)


def solution(mesh):
    in_specs = (P("tm", "chan"), P(None, "tm", "chan"))
    out_specs = P(None, ("tm", "chan"))
    return jax.shard_map(local, mesh=mesh, in_specs=in_specs, out_specs=out_specs, check_vma=False)
```

```python
import math

import jax
import jax.numpy as jnp
from jax import lax
from jax.experimental import pallas as pl
from jax.experimental.pallas import tpu as pltpu
from jax.sharding import PartitionSpec as P

CH = 10240
L = 256
K = 16
SUB = 8
ROWS = 1024
RIM = 256
USED = ROWS + 16
SPAN = ROWS + 128
EDGE_USED = RIM + 16
EDGE_SPAN = RIM + 128
NN = (((1,), (0,)), ((), ()))
BF16 = jnp.bfloat16
VMEM = pl.BlockSpec(memory_space=pltpu.VMEM)
SMEM = pl.BlockSpec(memory_space=pltpu.SMEM)
ANY = pl.BlockSpec(memory_space=pl.ANY)


def swap(v):
    return jnp.concatenate([v[:, 64:], v[:, :64]], axis=1)


def low_lanes():
    return lax.broadcasted_iota(jnp.int32, (1, 128), 1) < 64


def pack_rest(v, half):
    n = v.shape[0] // 2
    if half == 0:
        return jnp.where(low_lanes(), v[:n], swap(v[n:]))
    return jnp.where(low_lanes(), swap(v[:n]), v[n:])


def pack_half(v, half, upper):
    return [
        jnp.where(upper, v[:, 256:384], v[:, 0:128]),
        jnp.where(upper, v[:, 384:512], v[:, 128:256]),
        jnp.where(upper, pack_rest(v[:, 512:640], 1), pack_rest(v[:, 512:640], 0)),
    ]


def first_pack_kernel(place, x, send):
    at = 0
    for part in pack_half(x[...], None, place[1] == 0):
        send[at : at + part.shape[0]] = part
        at += part.shape[0]


def lag_pack_kernel(lags, copies, packed, sems):
    i = lax.broadcasted_iota(jnp.int32, (K * SUB, K * SUB), 0)
    j = lax.broadcasted_iota(jnp.int32, (K * SUB, K * SUB), 1)
    order = (i // SUB * SUB + (SUB - 1 - i % SUB) == j).astype(BF16)
    v = lax.dot_general(order, lags[...], NN, preferred_element_type=jnp.float32).astype(BF16)
    for half in range(2):
        packed[half, 0:128] = v[:, 256 * half : 256 * half + 128]
        packed[half, 128:256] = v[:, 256 * half + 128 : 256 * half + 256]
        packed[half, 256:320] = pack_rest(v[:, 512:640], half)
    moves = [pltpu.make_async_copy(packed.at[p // 8], copies.at[p], sems.at[p]) for p in range(16)]
    for move in moves:
        move.start()
    for move in moves:
        move.wait()


def first_pack(place, x):
    return pl.pallas_call(
        first_pack_kernel,
        out_shape=jax.ShapeDtypeStruct((ROWS * 5 // 2, 128), BF16),
        in_specs=[SMEM, VMEM],
        out_specs=VMEM,
        compiler_params=pltpu.CompilerParams(vmem_limit_bytes=16 * 2**20),
        cost_estimate=pl.CostEstimate(flops=2_000_000, bytes_accessed=2_000_000, transcendentals=0),
        name="first_pack",
    )(place, x)


def lag_pack(lags):
    return pl.pallas_call(
        lag_pack_kernel,
        out_shape=jax.ShapeDtypeStruct((16, 320, 128), BF16),
        in_specs=[VMEM],
        out_specs=ANY,
        scratch_shapes=[pltpu.VMEM((2, 320, 128), BF16), pltpu.SemaphoreType.DMA((16,))],
        cost_estimate=pl.CostEstimate(flops=2_000_000, bytes_accessed=1_500_000, transcendentals=0),
        name="lag_pack",
    )(lags)


def lanes_of(half, c):
    return pl.ds(pl.multiple_of(256 * half + 128 * c, 128), 128)


def lag_pair(ref, even, odd):
    pe, po = ref[even, 256:320], ref[odd, 256:320]
    rest = jnp.concatenate(
        [jnp.where(low_lanes(), pe, swap(po)), jnp.where(low_lanes(), swap(pe), po)], axis=0
    )
    return jnp.concatenate(
        [ref[even, 0:128], ref[even, 128:256], ref[odd, 0:128], ref[odd, 128:256], rest], axis=1
    )


def sum_lags(xm, x2, q, own, oth, used, with_energy):
    te = jnp.zeros((2 * K * SUB, 128), jnp.float32)
    for s in range(2):
        ws = []
        for a in range(4 * s, 4 * s + 4):
            w = jnp.concatenate([lag_pair(ref, 2 * a, 2 * a + 1) for ref in (own, oth)], axis=0)
            if with_energy:
                wf = w.astype(jnp.float32)
                sq = wf * wf
                for j in range(5):
                    te = te + sq[:, 128 * j : 128 * j + 128]
            for j in range(5):
                ws.append(jnp.transpose(w[:, 128 * j : 128 * j + 128]))
        w = jnp.concatenate(ws, axis=0)
        for b in range(2):
            rows = []
            for a in range(4 * s, 4 * s + 4):
                r = 32 * a
                rows += [xm[b, r : r + used], xm[b, r + 16 : r + 16 + used], x2[b, r : r + used]]
            part = lax.dot_general(jnp.concatenate(rows, axis=1), w, NN, preferred_element_type=jnp.float32)
            q[b, 0:used, :] = part if s == 0 else q[b, 0:used, :] + part
    te = jnp.sum(te.reshape(2, K, SUB, 128), axis=(0, 2))
    te = jnp.sum(te, axis=1, keepdims=True)
    lane = lax.broadcasted_iota(jnp.int32, (K, 128), 1)
    row = lax.broadcasted_iota(jnp.int32, (K, 128), 0)
    return jnp.sum(jnp.where(lane == 64 + row, te, 0.0), axis=0, keepdims=True)


def sum_fine_lags(q, b, span, used, z):
    q[b, used:span, :] = jnp.zeros((span - used, 2 * K * SUB), jnp.float32)
    sums = []
    for g in range(2):
        p = jnp.transpose(q[b, :, 128 * g : 128 * g + 128])
        p = p.reshape(K, SUB, span)
        p = pltpu.roll(p, span - (SUB - 1), 2, stride=1, stride_axis=1)
        sums.append(jnp.sum(p, axis=1))
    late = [pltpu.roll(p, span - SUB, 1) for p in sums]
    return jnp.where(z == 1, late[0] + sums[1], sums[0] + late[1])


def window_energy(xm, x2, b, n):
    sq = jnp.zeros((n, 128), jnp.float32)
    rest = x2[b, 0:n]
    for v in (xm[b, 0:n, 0:128], xm[b, 0:n, 128:256], jnp.where(low_lanes(), rest, jnp.zeros_like(rest))):
        v = v.astype(jnp.float32)
        sq = sq + v * v
    de = jnp.sum(jnp.transpose(sq), axis=0, keepdims=True)
    de = jnp.broadcast_to(de, (8, n))
    for i in range(8):
        de = de + pltpu.roll(de, n - (1 << i), 1)
    return de


def store(out, at, stack, de, te_row, count):
    low = low_lanes()
    for d in range(count):
        tile = slice(128 * (d // 2), 128 * (d // 2) + 128)
        lo, hi, en = stack[0:8, tile], stack[8:16, tile], de[:, tile]
        if d % 2 == 0:
            hi = pltpu.roll(hi, 64, 1)
        else:
            lo, en = pltpu.roll(lo, 64, 1), pltpu.roll(en, 64, 1)
        both = jnp.where(low, lo, hi)
        for r in range(8):
            out[at + d, :, 128 * r : 128 * r + 128] = both[r : r + 1]
        out[at + d, :, 1024:1152] = jnp.where(low, en[0:1], te_row)


def lay_out_rest(x2, b, left, right, before, after):
    zeros = [jnp.zeros((n, 128), BF16) for n in (before, after)]
    left = jnp.concatenate([v for v in (zeros[0], left, zeros[1]) if v.shape[0]], axis=0)
    right = jnp.concatenate([v for v in (zeros[0], right, zeros[1]) if v.shape[0]], axis=0)
    n = left.shape[0]
    x2[b, 0 : n - 16] = jnp.where(low_lanes(), left[0 : n - 16], right[16:n])
    x2[b, n - 16 : n] = jnp.where(low_lanes(), left[n - 16 : n], jnp.zeros((16, 128), BF16))


def fetch(x, got, own, oth, half, rows, at, xm, mine, his, lo_lags, hi_lags, sems):
    first = [
        pltpu.make_async_copy(x.at[pl.ds(0, rows), pl.ds(512, 128)], mine, sems.at[0]),
        pltpu.make_async_copy(got.at[pl.ds(2 * ROWS, his.shape[0])], his, sems.at[1]),
    ]
    second = [
        pltpu.make_async_copy(own, lo_lags, sems.at[2]),
        pltpu.make_async_copy(oth, hi_lags, sems.at[3]),
    ]
    for c in range(2):
        lanes, body = pl.ds(128 * c, 128), pl.ds(at, rows)
        second += [
            pltpu.make_async_copy(x.at[pl.ds(0, rows), lanes_of(half, c)], xm.at[0, body, lanes], sems.at[4 + c]),
            pltpu.make_async_copy(got.at[pl.ds(ROWS * c, rows)], xm.at[1, body, lanes], sems.at[6 + c]),
        ]
    for move in first + second:
        move.start()
    return first, second


def edge_kernel(place, x, got, own, oth, edges, xm, x2, q, mine, his, lo_lags, hi_lags, sums, sems):
    z, half = place[0], place[1]
    first, second = fetch(x, got, own, oth, half, RIM, RIM, xm, mine, his, lo_lags, hi_lags, sems)
    for move in first:
        move.wait()
    for b in range(2):
        xm[b, 0:RIM] = jnp.zeros((RIM, 256), BF16)
        if b == 0:
            v = mine[...]
            left, right = jnp.where(half == 1, swap(v), v), jnp.where(half == 1, v, swap(v))
        else:
            p = his[...]
            left, right = p, swap(p)
        lay_out_rest(x2, b, left, right, RIM, 0)
    for move in second:
        move.wait()
    sum_lags(xm, x2, q, lo_lags, hi_lags, EDGE_USED, False)
    for b in range(2):
        stack = sum_fine_lags(q, b, EDGE_SPAN, EDGE_USED, z)
        de = window_energy(xm, x2, b, 2 * RIM)
        store(sums, 4 * b, stack, de, jnp.zeros((1, 128), jnp.float32), 4)
    low = jnp.where(half == 1, sums[4:8], sums[0:4])
    high = jnp.where(half == 1, sums[0:4], sums[4:8])
    turn = place[2] == 1
    edges[0:4] = jnp.where(turn, high, low)
    edges[4:8] = jnp.where(turn, jnp.zeros_like(high), high)


def main_kernel(place, x, got, own, oth, out, xm, x2, q, mine, his, lo_lags, hi_lags, sems):
    z, half = place[0], place[1]
    first, second = fetch(x, got, own, oth, half, ROWS, 0, xm, mine, his, lo_lags, hi_lags, sems)
    for move in first:
        move.wait()
    for b in range(2):
        xm[b, ROWS:] = jnp.zeros((RIM, 256), BF16)
        if b == 0:
            v = mine[...]
            left, right = jnp.where(half == 1, swap(v), v), jnp.where(half == 1, v, swap(v))
        else:
            p = his[...]
            left, right = jnp.concatenate([p, swap(p)], axis=0), jnp.concatenate([swap(p), p], axis=0)
        lay_out_rest(x2, b, left, right, 0, RIM)
    for move in second:
        move.wait()
    te_row = sum_lags(xm, x2, q, lo_lags, hi_lags, USED, True)
    for b in range(2):
        stack = sum_fine_lags(q, b, SPAN, USED, z)
        de = window_energy(xm, x2, b, ROWS + RIM)
        store(out, 16 * jnp.where(half == b, 0, 1), stack, de, te_row, 16)


def scratch(rows, span, his_rows):
    return [
        pltpu.VMEM((2, rows + RIM, 256), BF16),
        pltpu.VMEM((2, rows + RIM, 128), BF16),
        pltpu.VMEM((2, span, 2 * K * SUB), jnp.float32),
        pltpu.VMEM((rows, 128), BF16),
        pltpu.VMEM((his_rows, 128), BF16),
        pltpu.VMEM((16, 320, 128), BF16),
        pltpu.VMEM((16, 320, 128), BF16),
    ]


def edge_sums(*args):
    return pl.pallas_call(
        edge_kernel,
        out_shape=jax.ShapeDtypeStruct((8, 1, 1152), jnp.float32),
        in_specs=[SMEM] + [ANY] * 4,
        out_specs=VMEM,
        scratch_shapes=scratch(RIM, EDGE_SPAN, RIM)
        + [pltpu.VMEM((8, 1, 1152), jnp.float32), pltpu.SemaphoreType.DMA((8,))],
        compiler_params=pltpu.CompilerParams(vmem_limit_bytes=32 * 2**20),
        cost_estimate=pl.CostEstimate(flops=1_400_000_000, bytes_accessed=3_200_000, transcendentals=0),
        name="edge_sums",
    )(*args)


def main_sums(*args):
    return pl.pallas_call(
        main_kernel,
        out_shape=jax.ShapeDtypeStruct((32, 1, 1152), jnp.float32),
        in_specs=[SMEM] + [ANY] * 4,
        out_specs=VMEM,
        scratch_shapes=scratch(ROWS, SPAN, ROWS // 2) + [pltpu.SemaphoreType.DMA((8,))],
        compiler_params=pltpu.CompilerParams(vmem_limit_bytes=48 * 2**20),
        cost_estimate=pl.CostEstimate(flops=5_500_000_000, bytes_accessed=5_000_000, transcendentals=0),
        name="main_sums",
    )(*args)


def finish_kernel(parts, out):
    total = jnp.sum(parts[...], axis=0)
    scale = math.sqrt(L * CH)
    rows = jnp.concatenate([total[:, 128 * r : 128 * r + 128] for r in range(8)], axis=0)
    last = total[:, 1024:1152]
    lane = lax.broadcasted_iota(jnp.int32, (K, 128), 1)
    row = lax.broadcasted_iota(jnp.int32, (K, 128), 0)
    te = jnp.sum(jnp.where(lane == 64 + row, last, 0.0), axis=1, keepdims=True)
    both = jnp.concatenate([rows[:, 0:64], rows[:, 64:128]], axis=0)
    out[...] = both * scale * lax.rsqrt(last[:, 0:64] + 1e-06) * lax.rsqrt(te)


def finish(parts):
    return pl.pallas_call(
        finish_kernel,
        out_shape=jax.ShapeDtypeStruct((K, 64), jnp.float32),
        in_specs=[VMEM],
        out_specs=VMEM,
        name="finish",
    )(parts)


def local(waveform, templates):
    tm = lax.axis_size("tm")
    chan = lax.axis_size("chan")
    me = lax.axis_index("tm")
    half = me // 16
    turn = jnp.logical_and(lax.rem(me, 8) == 0, lax.rem(me // 8, 2) == 0)
    place = jnp.stack([lax.rem(me, 2), half, turn.astype(jnp.int32)])
    plane = [[2 * i + h for i in range(tm // 2)] for h in range(2)]
    partner = [(i, i ^ 16) for i in range(tm)]

    shard = templates.reshape(K * SUB, -1)
    other = lax.ppermute(shard, "tm", [(i, i ^ 1) for i in range(tm)])
    got = lax.ppermute(first_pack(place, waveform), "tm", partner)

    def exchange(copies):
        return lax.all_to_all(copies, "tm", 0, 0, axis_index_groups=plane)

    own = lax.cond(me // tm == 0, exchange, lambda copies: copies, lag_pack(shard))
    other, got, own = lax.optimization_barrier((other, got, own))
    oth = exchange(lag_pack(other))

    edges = edge_sums(place, waveform, got, own, oth)
    edges = lax.ppermute(edges, "tm", [(i, i - 1 if i % 8 else (i ^ 8) + 7) for i in range(tm)])

    parts = main_sums(place, waveform, got, own, oth)
    edges = jnp.pad(edges.reshape(2, 4, 1, 1152), ((0, 0), (12, 0), (0, 0), (0, 0)))
    parts = parts + edges.reshape(parts.shape)
    pairs = [[t * chan + c for t in (i, i ^ 16) for c in range(chan)] for i in range(tm // 2)]
    parts = lax.all_to_all(parts, ("tm", "chan"), 0, 0, axis_index_groups=pairs)
    return finish(parts)


def solution(mesh):
    in_specs = (P("tm", "chan"), P(None, "tm", "chan"))
    out_specs = P(None, ("tm", "chan"))
    return jax.shard_map(local, mesh=mesh, in_specs=in_specs, out_specs=out_specs, check_vma=False)
```

```python
import math

import jax
import jax.numpy as jnp
from jax import lax
from jax.experimental import pallas as pl
from jax.experimental.pallas import tpu as pltpu
from jax.sharding import PartitionSpec as P

CH = 10240
L = 256
K = 16
SUB = 8
ROWS = 1024
RIM = 256
USED = ROWS + 16
SPAN = ROWS + 128
EDGE_USED = RIM + 16
EDGE_SPAN = RIM + 128
NN = (((1,), (0,)), ((), ()))
BF16 = jnp.bfloat16
VMEM = pl.BlockSpec(memory_space=pltpu.VMEM)
SMEM = pl.BlockSpec(memory_space=pltpu.SMEM)
ANY = pl.BlockSpec(memory_space=pl.ANY)


def swap(v):
    return jnp.concatenate([v[:, 64:], v[:, :64]], axis=1)


def low_lanes():
    return lax.broadcasted_iota(jnp.int32, (1, 128), 1) < 64


def pack_rest(v, half):
    n = v.shape[0] // 2
    if half == 0:
        return jnp.where(low_lanes(), v[:n], swap(v[n:]))
    return jnp.where(low_lanes(), swap(v[:n]), v[n:])


def first_pack_kernel(place, x, send, rest, sems):
    other = 1 - place[1]
    moves = [
        pltpu.make_async_copy(x.at[:, pl.ds(512, 128)], rest, sems.at[0]),
        pltpu.make_async_copy(x.at[:, lanes_of(other, 0)], send.at[pl.ds(0, ROWS)], sems.at[1]),
        pltpu.make_async_copy(x.at[:, lanes_of(other, 1)], send.at[pl.ds(ROWS, ROWS)], sems.at[2]),
    ]
    for move in moves:
        move.start()
    moves[0].wait()
    v = rest[...]
    send[2 * ROWS :] = jnp.where(other == 1, pack_rest(v, 1), pack_rest(v, 0))
    for move in moves[1:]:
        move.wait()


def lag_pack_kernel(lags, copies):
    i = lax.broadcasted_iota(jnp.int32, (K * SUB, K * SUB), 0)
    j = lax.broadcasted_iota(jnp.int32, (K * SUB, K * SUB), 1)
    order = (i // SUB * SUB + (SUB - 1 - i % SUB) == j).astype(BF16)
    v = lax.dot_general(order, lags[...], NN, preferred_element_type=jnp.float32).astype(BF16)
    for half in range(2):
        first, second = v[:, 256 * half : 256 * half + 128], v[:, 256 * half + 128 : 256 * half + 256]
        rest = pack_rest(v[:, 512:640], half)
        for p in range(8 * half, 8 * half + 8):
            copies[p, 0:128] = first
            copies[p, 128:256] = second
            copies[p, 256:320] = rest


def first_pack(place, x):
    return pl.pallas_call(
        first_pack_kernel,
        out_shape=jax.ShapeDtypeStruct((ROWS * 5 // 2, 128), BF16),
        in_specs=[SMEM, ANY],
        out_specs=VMEM,
        scratch_shapes=[pltpu.VMEM((ROWS, 128), BF16), pltpu.SemaphoreType.DMA((3,))],
        compiler_params=pltpu.CompilerParams(vmem_limit_bytes=8 * 2**20),
        cost_estimate=pl.CostEstimate(flops=2_000_000, bytes_accessed=2_000_000, transcendentals=0),
        name="first_pack",
    )(place, x)


def lag_pack(lags):
    return pl.pallas_call(
        lag_pack_kernel,
        out_shape=jax.ShapeDtypeStruct((16, 320, 128), BF16),
        in_specs=[VMEM],
        out_specs=VMEM,
        compiler_params=pltpu.CompilerParams(vmem_limit_bytes=8 * 2**20),
        cost_estimate=pl.CostEstimate(flops=2_000_000, bytes_accessed=1_500_000, transcendentals=0),
        name="lag_pack",
    )(lags)


def lanes_of(half, c):
    return pl.ds(pl.multiple_of(256 * half + 128 * c, 128), 128)


def lag_pair(ref, even, odd):
    pe, po = ref[even, 256:320], ref[odd, 256:320]
    rest = jnp.concatenate(
        [jnp.where(low_lanes(), pe, swap(po)), jnp.where(low_lanes(), swap(pe), po)], axis=0
    )
    return jnp.concatenate(
        [ref[even, 0:128], ref[even, 128:256], ref[odd, 0:128], ref[odd, 128:256], rest], axis=1
    )


def sum_lags(xm, x2, q, own, oth, used, with_energy):
    te = jnp.zeros((2 * K * SUB, 128), jnp.float32)
    for s in range(2):
        ws = []
        for a in range(4 * s, 4 * s + 4):
            w = jnp.concatenate([lag_pair(ref, 2 * a, 2 * a + 1) for ref in (own, oth)], axis=0)
            if with_energy:
                wf = w.astype(jnp.float32)
                sq = wf * wf
                for j in range(5):
                    te = te + sq[:, 128 * j : 128 * j + 128]
            for j in range(5):
                ws.append(jnp.transpose(w[:, 128 * j : 128 * j + 128]))
        w = jnp.concatenate(ws, axis=0)
        for b in range(2):
            rows = []
            for a in range(4 * s, 4 * s + 4):
                r = 32 * a
                rows += [xm[b, r : r + used], xm[b, r + 16 : r + 16 + used], x2[b, r : r + used]]
            part = lax.dot_general(jnp.concatenate(rows, axis=1), w, NN, preferred_element_type=jnp.float32)
            q[b, 0:used, :] = part if s == 0 else q[b, 0:used, :] + part
    te = jnp.sum(te.reshape(2, K, SUB, 128), axis=(0, 2))
    te = jnp.sum(te, axis=1, keepdims=True)
    lane = lax.broadcasted_iota(jnp.int32, (K, 128), 1)
    row = lax.broadcasted_iota(jnp.int32, (K, 128), 0)
    return jnp.sum(jnp.where(lane == 64 + row, te, 0.0), axis=0, keepdims=True)


def sum_fine_lags(q, b, span, used, z):
    q[b, used:span, :] = jnp.zeros((span - used, 2 * K * SUB), jnp.float32)
    sums = []
    for g in range(2):
        p = jnp.transpose(q[b, :, 128 * g : 128 * g + 128])
        p = p.reshape(K, SUB, span)
        p = pltpu.roll(p, span - (SUB - 1), 2, stride=1, stride_axis=1)
        sums.append(jnp.sum(p, axis=1))
    late = [pltpu.roll(p, span - SUB, 1) for p in sums]
    return jnp.where(z == 1, late[0] + sums[1], sums[0] + late[1])


def window_energy(xm, x2, b, n):
    sq = jnp.zeros((n, 128), jnp.float32)
    rest = x2[b, 0:n]
    for v in (xm[b, 0:n, 0:128], xm[b, 0:n, 128:256], jnp.where(low_lanes(), rest, jnp.zeros_like(rest))):
        v = v.astype(jnp.float32)
        sq = sq + v * v
    de = jnp.sum(jnp.transpose(sq), axis=0, keepdims=True)
    de = jnp.broadcast_to(de, (8, n))
    for i in range(8):
        de = de + pltpu.roll(de, n - (1 << i), 1)
    return de


def store(out, at, stack, de, te_row, count):
    low = low_lanes()
    for d in range(count):
        tile = slice(128 * (d // 2), 128 * (d // 2) + 128)
        lo, hi, en = stack[0:8, tile], stack[8:16, tile], de[:, tile]
        if d % 2 == 0:
            hi = pltpu.roll(hi, 64, 1)
        else:
            lo, en = pltpu.roll(lo, 64, 1), pltpu.roll(en, 64, 1)
        both = jnp.where(low, lo, hi)
        for r in range(8):
            out[at + d, :, 128 * r : 128 * r + 128] = both[r : r + 1]
        out[at + d, :, 1024:1152] = jnp.where(low, en[0:1], te_row)


def lay_out_rest(x2, b, left, right, before, after):
    zeros = [jnp.zeros((n, 128), BF16) for n in (before, after)]
    left = jnp.concatenate([v for v in (zeros[0], left, zeros[1]) if v.shape[0]], axis=0)
    right = jnp.concatenate([v for v in (zeros[0], right, zeros[1]) if v.shape[0]], axis=0)
    n = left.shape[0]
    x2[b, 0 : n - 16] = jnp.where(low_lanes(), left[0 : n - 16], right[16:n])
    x2[b, n - 16 : n] = jnp.where(low_lanes(), left[n - 16 : n], jnp.zeros((16, 128), BF16))


def fetch(x, got, half, rows, at, xm, mine, his, sems):
    first = [
        pltpu.make_async_copy(x.at[pl.ds(0, rows), pl.ds(512, 128)], mine, sems.at[0]),
        pltpu.make_async_copy(got.at[pl.ds(2 * ROWS, his.shape[0])], his, sems.at[1]),
    ]
    second = []
    for c in range(2):
        lanes, body = pl.ds(128 * c, 128), pl.ds(at, rows)
        second += [
            pltpu.make_async_copy(x.at[pl.ds(0, rows), lanes_of(half, c)], xm.at[0, body, lanes], sems.at[2 + c]),
            pltpu.make_async_copy(got.at[pl.ds(ROWS * c, rows)], xm.at[1, body, lanes], sems.at[4 + c]),
        ]
    for move in first + second:
        move.start()
    return first, second


def edge_kernel(place, x, got, own, oth, edges, xm, x2, q, mine, his, sums, sems):
    z, half = place[0], place[1]
    first, second = fetch(x, got, half, RIM, RIM, xm, mine, his, sems)
    for move in first:
        move.wait()
    for b in range(2):
        xm[b, 0:RIM] = jnp.zeros((RIM, 256), BF16)
        if b == 0:
            v = mine[...]
            left, right = jnp.where(half == 1, swap(v), v), jnp.where(half == 1, v, swap(v))
        else:
            p = his[...]
            left, right = p, swap(p)
        lay_out_rest(x2, b, left, right, RIM, 0)
    for move in second:
        move.wait()
    sum_lags(xm, x2, q, own, oth, EDGE_USED, False)
    for b in range(2):
        stack = sum_fine_lags(q, b, EDGE_SPAN, EDGE_USED, z)
        de = window_energy(xm, x2, b, 2 * RIM)
        store(sums, 4 * b, stack, de, jnp.zeros((1, 128), jnp.float32), 4)
    low = jnp.where(half == 1, sums[4:8], sums[0:4])
    high = jnp.where(half == 1, sums[0:4], sums[4:8])
    turn = place[2] == 1
    edges[0:4] = jnp.where(turn, high, low)
    edges[4:8] = jnp.where(turn, jnp.zeros_like(high), high)


def main_kernel(place, x, got, own, oth, out, xm, x2, q, mine, his, sems):
    z, half = place[0], place[1]
    first, second = fetch(x, got, half, ROWS, 0, xm, mine, his, sems)
    for move in first:
        move.wait()
    for b in range(2):
        xm[b, ROWS:] = jnp.zeros((RIM, 256), BF16)
        if b == 0:
            v = mine[...]
            left, right = jnp.where(half == 1, swap(v), v), jnp.where(half == 1, v, swap(v))
        else:
            p = his[...]
            left, right = jnp.concatenate([p, swap(p)], axis=0), jnp.concatenate([swap(p), p], axis=0)
        lay_out_rest(x2, b, left, right, 0, RIM)
    for move in second:
        move.wait()
    te_row = sum_lags(xm, x2, q, own, oth, USED, True)
    for b in range(2):
        stack = sum_fine_lags(q, b, SPAN, USED, z)
        de = window_energy(xm, x2, b, ROWS + RIM)
        store(out, 16 * jnp.where(half == b, 0, 1), stack, de, te_row, 16)


def scratch(rows, span, his_rows):
    return [
        pltpu.VMEM((2, rows + RIM, 256), BF16),
        pltpu.VMEM((2, rows + RIM, 128), BF16),
        pltpu.VMEM((2, span, 2 * K * SUB), jnp.float32),
        pltpu.VMEM((rows, 128), BF16),
        pltpu.VMEM((his_rows, 128), BF16),
    ]


def edge_sums(*args):
    return pl.pallas_call(
        edge_kernel,
        out_shape=jax.ShapeDtypeStruct((8, 1, 1152), jnp.float32),
        in_specs=[SMEM, ANY, ANY, VMEM, VMEM],
        out_specs=VMEM,
        scratch_shapes=scratch(RIM, EDGE_SPAN, RIM)
        + [pltpu.VMEM((8, 1, 1152), jnp.float32), pltpu.SemaphoreType.DMA((6,))],
        compiler_params=pltpu.CompilerParams(vmem_limit_bytes=20 * 2**20),
        cost_estimate=pl.CostEstimate(flops=1_400_000_000, bytes_accessed=3_200_000, transcendentals=0),
        name="edge_sums",
    )(*args)


def main_sums(*args):
    return pl.pallas_call(
        main_kernel,
        out_shape=jax.ShapeDtypeStruct((32, 1, 1152), jnp.float32),
        in_specs=[SMEM, ANY, ANY, VMEM, VMEM],
        out_specs=VMEM,
        scratch_shapes=scratch(ROWS, SPAN, ROWS // 2) + [pltpu.SemaphoreType.DMA((6,))],
        compiler_params=pltpu.CompilerParams(vmem_limit_bytes=48 * 2**20),
        cost_estimate=pl.CostEstimate(flops=5_500_000_000, bytes_accessed=5_000_000, transcendentals=0),
        name="main_sums",
    )(*args)


def finish_kernel(parts, out):
    total = jnp.sum(parts[...], axis=0)
    scale = math.sqrt(L * CH)
    rows = jnp.concatenate([total[:, 128 * r : 128 * r + 128] for r in range(8)], axis=0)
    last = total[:, 1024:1152]
    lane = lax.broadcasted_iota(jnp.int32, (K, 128), 1)
    row = lax.broadcasted_iota(jnp.int32, (K, 128), 0)
    te = jnp.sum(jnp.where(lane == 64 + row, last, 0.0), axis=1, keepdims=True)
    both = jnp.concatenate([rows[:, 0:64], rows[:, 64:128]], axis=0)
    out[...] = both * scale * lax.rsqrt(last[:, 0:64] + 1e-06) * lax.rsqrt(te)


def finish(parts):
    return pl.pallas_call(
        finish_kernel,
        out_shape=jax.ShapeDtypeStruct((K, 64), jnp.float32),
        in_specs=[VMEM],
        out_specs=VMEM,
        compiler_params=pltpu.CompilerParams(vmem_limit_bytes=4 * 2**20),
        name="finish",
    )(parts)


def local(waveform, templates):
    tm = lax.axis_size("tm")
    chan = lax.axis_size("chan")
    me = lax.axis_index("tm")
    half = me // 16
    turn = jnp.logical_and(lax.rem(me, 8) == 0, lax.rem(me // 8, 2) == 0)
    place = jnp.stack([lax.rem(me, 2), half, turn.astype(jnp.int32)])
    plane = [[2 * i + h for i in range(tm // 2)] for h in range(2)]
    partner = [(i, i ^ 16) for i in range(tm)]

    shard = templates.reshape(K * SUB, -1)
    other = lax.ppermute(shard, "tm", [(i, i ^ 1) for i in range(tm)])
    got = lax.ppermute(first_pack(place, waveform), "tm", partner)

    def exchange(copies):
        return lax.all_to_all(copies, "tm", 0, 0, axis_index_groups=plane)

    own = lax.cond(me // tm == 0, exchange, lambda copies: copies, lag_pack(shard))
    other, got, own = lax.optimization_barrier((other, got, own))
    oth = exchange(lag_pack(other))

    edges = edge_sums(place, waveform, got, own, oth)
    edges = lax.ppermute(edges, "tm", [(i, i - 1 if i % 8 else (i ^ 8) + 7) for i in range(tm)])

    parts = main_sums(place, waveform, got, own, oth)
    edges = jnp.pad(edges.reshape(2, 4, 1, 1152), ((0, 0), (12, 0), (0, 0), (0, 0)))
    parts = parts + edges.reshape(parts.shape)
    pairs = [[t * chan + c for t in (i, i ^ 16) for c in range(chan)] for i in range(tm // 2)]
    parts = lax.all_to_all(parts, ("tm", "chan"), 0, 0, axis_index_groups=pairs)
    return finish(parts)


def solution(mesh):
    in_specs = (P("tm", "chan"), P(None, "tm", "chan"))
    out_specs = P(None, ("tm", "chan"))
    return jax.shard_map(local, mesh=mesh, in_specs=in_specs, out_specs=out_specs, check_vma=False)
```

```python
import math

import jax
import jax.numpy as jnp
from jax import lax
from jax.experimental import pallas as pl
from jax.experimental.pallas import tpu as pltpu
from jax.sharding import PartitionSpec as P

CH = 10240
L = 256
K = 16
SUB = 8
ROWS = 1024
RIM = 256
USED = ROWS + 16
SPAN = ROWS + 128
EDGE_USED = RIM + 16
EDGE_SPAN = RIM + 128
NN = (((1,), (0,)), ((), ()))
BF16 = jnp.bfloat16
VMEM = pl.BlockSpec(memory_space=pltpu.VMEM)
SMEM = pl.BlockSpec(memory_space=pltpu.SMEM)
ANY = pl.BlockSpec(memory_space=pl.ANY)


def swap(v):
    return jnp.concatenate([v[:, 64:], v[:, :64]], axis=1)


def low_lanes():
    return lax.broadcasted_iota(jnp.int32, (1, 128), 1) < 64


def pack_rest(v, half):
    n = v.shape[0] // 2
    if half == 0:
        return jnp.where(low_lanes(), v[:n], swap(v[n:]))
    return jnp.where(low_lanes(), swap(v[:n]), v[n:])


def first_pack_kernel(place, x, send, rest, sems):
    other = 1 - place[1]
    moves = [
        pltpu.make_async_copy(x.at[:, pl.ds(512, 128)], rest, sems.at[0]),
        pltpu.make_async_copy(x.at[:, lanes_of(other, 0)], send.at[pl.ds(0, ROWS)], sems.at[1]),
        pltpu.make_async_copy(x.at[:, lanes_of(other, 1)], send.at[pl.ds(ROWS, ROWS)], sems.at[2]),
    ]
    for move in moves:
        move.start()
    moves[0].wait()
    v = rest[...]
    send[2 * ROWS :] = jnp.where(other == 1, pack_rest(v, 1), pack_rest(v, 0))
    for move in moves[1:]:
        move.wait()


def lag_pack_kernel(lags, copies):
    i = lax.broadcasted_iota(jnp.int32, (K * SUB, K * SUB), 0)
    j = lax.broadcasted_iota(jnp.int32, (K * SUB, K * SUB), 1)
    order = (i // SUB * SUB + (SUB - 1 - i % SUB) == j).astype(BF16)
    v = lax.dot_general(order, lags[...], NN, preferred_element_type=jnp.float32).astype(BF16)
    for half in range(2):
        first, second = v[:, 256 * half : 256 * half + 128], v[:, 256 * half + 128 : 256 * half + 256]
        rest = pack_rest(v[:, 512:640], half)
        for p in range(16):
            if p // 4 % 2 == half:
                copies[p, 0:128] = first
                copies[p, 128:256] = second
                copies[p, 256:320] = rest


def first_pack(place, x):
    return pl.pallas_call(
        first_pack_kernel,
        out_shape=jax.ShapeDtypeStruct((ROWS * 5 // 2, 128), BF16),
        in_specs=[SMEM, ANY],
        out_specs=VMEM,
        scratch_shapes=[pltpu.VMEM((ROWS, 128), BF16), pltpu.SemaphoreType.DMA((3,))],
        compiler_params=pltpu.CompilerParams(vmem_limit_bytes=4 * 2**20),
        cost_estimate=pl.CostEstimate(flops=2_000_000, bytes_accessed=2_000_000, transcendentals=0),
        name="first_pack",
    )(place, x)


def lag_pack(lags, flops=2_000_000):
    return pl.pallas_call(
        lag_pack_kernel,
        out_shape=jax.ShapeDtypeStruct((16, 320, 128), BF16),
        in_specs=[VMEM],
        out_specs=VMEM,
        compiler_params=pltpu.CompilerParams(vmem_limit_bytes=4 * 2**20),
        cost_estimate=pl.CostEstimate(flops=flops, bytes_accessed=1_500_000, transcendentals=0),
        name="lag_pack",
    )(lags)


def pack_half(v, upper):
    return [
        jnp.where(upper, v[:, 256:384], v[:, 0:128]),
        jnp.where(upper, v[:, 384:512], v[:, 128:256]),
        jnp.where(upper, pack_rest(v[:, 512:640], 1), pack_rest(v[:, 512:640], 0)),
    ]


def both_heads(place, x, got):
    rest = got[2 * ROWS : 2 * ROWS + RIM]
    theirs = [
        got[0:RIM],
        got[ROWS : ROWS + RIM],
        jnp.where(low_lanes(), rest[0 : RIM // 2], swap(rest[RIM // 2 :])),
    ]
    upper = place[1] == 1
    mine = pack_half(x, upper)
    even = [jnp.where(upper, b, a) for a, b in zip(mine, theirs)]
    odd = [jnp.where(upper, a, b) for a, b in zip(mine, theirs)]
    return even, odd


def head_kernel(x, low, high, rows, sem):
    move = pltpu.make_async_copy(x.at[pl.ds(0, RIM)], rows, sem.at[0])
    move.start()
    move.wait()
    v = rows[...]
    for half, out in enumerate((low, high)):
        out[0:RIM] = v[:, 256 * half : 256 * half + 128]
        out[RIM : 2 * RIM] = v[:, 256 * half + 128 : 256 * half + 256]
        out[2 * RIM :] = pack_rest(v[:, 512:640], half)


def heads(x):
    one = jax.ShapeDtypeStruct((RIM * 5 // 2, 128), BF16)
    return pl.pallas_call(
        head_kernel,
        out_shape=(one, one),
        in_specs=[ANY],
        out_specs=(VMEM, VMEM),
        scratch_shapes=[pltpu.VMEM((RIM, 640), BF16), pltpu.SemaphoreType.DMA((1,))],
        compiler_params=pltpu.CompilerParams(vmem_limit_bytes=4 * 2**20),
        cost_estimate=pl.CostEstimate(flops=2_000_000, bytes_accessed=700_000, transcendentals=0),
        name="heads",
    )(x)


def lanes_of(half, c):
    return pl.ds(pl.multiple_of(256 * half + 128 * c, 128), 128)


def lag_pair(ref, even, odd):
    pe, po = ref[even, 256:320], ref[odd, 256:320]
    rest = jnp.concatenate(
        [jnp.where(low_lanes(), pe, swap(po)), jnp.where(low_lanes(), swap(pe), po)], axis=0
    )
    return jnp.concatenate(
        [ref[even, 0:128], ref[even, 128:256], ref[odd, 0:128], ref[odd, 128:256], rest], axis=1
    )


def sum_lags(xm, x2, q, own, oth, used, with_energy):
    te = jnp.zeros((2 * K * SUB, 128), jnp.float32)
    for s in range(2):
        ws = []
        for a in range(4 * s, 4 * s + 4):
            w = jnp.concatenate([lag_pair(ref, 2 * a, 2 * a + 1) for ref in (own, oth)], axis=0)
            if with_energy:
                wf = w.astype(jnp.float32)
                sq = wf * wf
                for j in range(5):
                    te = te + sq[:, 128 * j : 128 * j + 128]
            for j in range(5):
                ws.append(jnp.transpose(w[:, 128 * j : 128 * j + 128]))
        w = jnp.concatenate(ws, axis=0)
        for b in range(2):
            rows = []
            for a in range(4 * s, 4 * s + 4):
                r = 32 * a
                rows += [xm[b, r : r + used], xm[b, r + 16 : r + 16 + used], x2[b, r : r + used]]
            part = lax.dot_general(jnp.concatenate(rows, axis=1), w, NN, preferred_element_type=jnp.float32)
            q[b, 0:used, :] = part if s == 0 else q[b, 0:used, :] + part
    te = jnp.sum(te.reshape(2, K, SUB, 128), axis=(0, 2))
    te = jnp.sum(te, axis=1, keepdims=True)
    lane = lax.broadcasted_iota(jnp.int32, (K, 128), 1)
    row = lax.broadcasted_iota(jnp.int32, (K, 128), 0)
    return jnp.sum(jnp.where(lane == 64 + row, te, 0.0), axis=0, keepdims=True)


def edge_lags(xm, x2, q, own, oth):
    parts = []
    for s, first in ((0, 144), (1, 16)):
        n = EDGE_USED - first
        ws, rows = [], []
        for a in range(4 * s, 4 * s + 4):
            ws.append(jnp.concatenate([lag_pair(ref, 2 * a, 2 * a + 1) for ref in (own, oth)], axis=0))
            r = 32 * a + first
            two = lambda ref, r: jnp.concatenate([ref[b, r : r + n] for b in range(2)], axis=0)
            rows += [two(xm, r), two(xm, r + 16), two(x2, r)]
        parts.append(
            lax.dot_general(
                jnp.concatenate(rows, axis=1),
                jnp.concatenate(ws, axis=1),
                (((1,), (1,)), ((), ())),
                preferred_element_type=jnp.float32,
            )
        )
    for b in range(2):
        q[b, 0:16, :] = jnp.zeros((16, 2 * K * SUB), jnp.float32)
        q[b, 16:144, :] = parts[1][256 * b : 256 * b + 128]
        q[b, 144:EDGE_USED, :] = parts[1][256 * b + 128 : 256 * b + 256] + parts[0][128 * b : 128 * b + 128]


def sum_fine_lags(q, b, span, used, z):
    q[b, used:span, :] = jnp.zeros((span - used, 2 * K * SUB), jnp.float32)
    sums = []
    for g in range(2):
        p = jnp.transpose(q[b, :, 128 * g : 128 * g + 128])
        p = p.reshape(K, SUB, span)
        p = pltpu.roll(p, span - (SUB - 1), 2, stride=1, stride_axis=1)
        sums.append(jnp.sum(p, axis=1))
    late = [pltpu.roll(p, span - SUB, 1) for p in sums]
    return jnp.where(z == 1, late[0] + sums[1], sums[0] + late[1])


def window_energy(xm, x2, b, n):
    sq = jnp.zeros((n, 128), jnp.float32)
    rest = x2[b, 0:n]
    for v in (xm[b, 0:n, 0:128], xm[b, 0:n, 128:256], jnp.where(low_lanes(), rest, jnp.zeros_like(rest))):
        v = v.astype(jnp.float32)
        sq = sq + v * v
    de = jnp.sum(jnp.transpose(sq), axis=0, keepdims=True)
    de = jnp.broadcast_to(de, (8, n))
    for i in range(8):
        de = de + pltpu.roll(de, n - (1 << i), 1)
    return de


def store(out, at, stack, de, te_row, count):
    low = low_lanes()
    for d in range(count):
        tile = slice(128 * (d // 2), 128 * (d // 2) + 128)
        lo, hi, en = stack[0:8, tile], stack[8:16, tile], de[:, tile]
        if d % 2 == 0:
            hi = pltpu.roll(hi, 64, 1)
        else:
            lo, en = pltpu.roll(lo, 64, 1), pltpu.roll(en, 64, 1)
        both = jnp.where(low, lo, hi)
        for r in range(8):
            out[at + d, :, 128 * r : 128 * r + 128] = both[r : r + 1]
        out[at + d, :, 1024:1152] = jnp.where(low, en[0:1], te_row)


def lay_out_rest(x2, b, left, right, before, after):
    zeros = [jnp.zeros((n, 128), BF16) for n in (before, after)]
    left = jnp.concatenate([v for v in (zeros[0], left, zeros[1]) if v.shape[0]], axis=0)
    right = jnp.concatenate([v for v in (zeros[0], right, zeros[1]) if v.shape[0]], axis=0)
    n = left.shape[0]
    x2[b, 0 : n - 16] = jnp.where(low_lanes(), left[0 : n - 16], right[16:n])
    x2[b, n - 16 : n] = jnp.where(low_lanes(), left[n - 16 : n], jnp.zeros((16, 128), BF16))


def fetch(x, got, half, rows, at, xm, mine, his, sems):
    first = [
        pltpu.make_async_copy(x.at[pl.ds(0, rows), pl.ds(512, 128)], mine, sems.at[0]),
        pltpu.make_async_copy(got.at[pl.ds(2 * ROWS, his.shape[0])], his, sems.at[1]),
    ]
    second = []
    for c in range(2):
        lanes, body = pl.ds(128 * c, 128), pl.ds(at, rows)
        second += [
            pltpu.make_async_copy(x.at[pl.ds(0, rows), lanes_of(half, c)], xm.at[0, body, lanes], sems.at[2 + c]),
            pltpu.make_async_copy(got.at[pl.ds(ROWS * c, rows)], xm.at[1, body, lanes], sems.at[4 + c]),
        ]
    for move in first + second:
        move.start()
    return first, second


def edge_kernel(place, x, got, third, own, oth, edges, xm, x2, q, rows, sem):
    move = pltpu.make_async_copy(x.at[pl.ds(0, RIM)], rows, sem.at[0])
    move.start()
    for b in range(2):
        xm[b, 0:RIM] = jnp.zeros((RIM, 256), BF16)
    move.wait()
    even, odd = both_heads(place, rows[...], got)
    turn = place[2] == 1
    after = [third[0:RIM], third[RIM : 2 * RIM], third[2 * RIM :]]
    heads = [
        [jnp.where(turn, n, v) for v, n in zip(even, odd)],
        [jnp.where(turn, n, v) for v, n in zip(odd, after)],
    ]
    for b in range(2):
        for c in range(2):
            xm[b, RIM:, 128 * c : 128 * c + 128] = heads[b][c]
        p = heads[b][2]
        left, right = jnp.concatenate([p, swap(p)], axis=0), jnp.concatenate([swap(p), p], axis=0)
        lay_out_rest(x2, b, left, right, RIM, 0)
    edge_lags(xm, x2, q, own, oth)
    for b in range(2):
        stack = sum_fine_lags(q, b, EDGE_SPAN, EDGE_USED, place[0])
        de = window_energy(xm, x2, b, 2 * RIM)
        store(edges, 4 * b, stack, de, jnp.zeros((1, 128), jnp.float32), 4)


def main_kernel(place, x, got, own, oth, out, xm, x2, q, mine, his, sems):
    z, half = place[0], place[1]
    first, second = fetch(x, got, half, ROWS, 0, xm, mine, his, sems)
    for move in first:
        move.wait()
    for b in range(2):
        xm[b, ROWS:] = jnp.zeros((RIM, 256), BF16)
        if b == 0:
            v = mine[...]
            left, right = jnp.where(half == 1, swap(v), v), jnp.where(half == 1, v, swap(v))
        else:
            p = his[...]
            left, right = jnp.concatenate([p, swap(p)], axis=0), jnp.concatenate([swap(p), p], axis=0)
        lay_out_rest(x2, b, left, right, 0, RIM)
    for move in second:
        move.wait()
    te_row = sum_lags(xm, x2, q, own, oth, USED, True)
    for b in range(2):
        stack = sum_fine_lags(q, b, SPAN, USED, z)
        de = window_energy(xm, x2, b, ROWS + RIM)
        store(out, 16 * jnp.where(half == b, 0, 1), stack, de, te_row, 16)


def scratch(rows, span, his_rows):
    return [
        pltpu.VMEM((2, rows + RIM, 256), BF16),
        pltpu.VMEM((2, rows + RIM, 128), BF16),
        pltpu.VMEM((2, span, 2 * K * SUB), jnp.float32),
        pltpu.VMEM((rows, 128), BF16),
        pltpu.VMEM((his_rows, 128), BF16),
    ]


def edge_sums(*args):
    return pl.pallas_call(
        edge_kernel,
        out_shape=jax.ShapeDtypeStruct((8, 1, 1152), jnp.float32),
        in_specs=[SMEM, ANY, VMEM, VMEM, VMEM, VMEM],
        out_specs=VMEM,
        scratch_shapes=[
            pltpu.VMEM((2, 2 * RIM, 256), BF16),
            pltpu.VMEM((2, 2 * RIM, 128), BF16),
            pltpu.VMEM((2, EDGE_SPAN, 2 * K * SUB), jnp.float32),
            pltpu.VMEM((RIM, 640), BF16),
            pltpu.SemaphoreType.DMA((1,)),
        ],
        compiler_params=pltpu.CompilerParams(vmem_limit_bytes=10 * 2**20),
        cost_estimate=pl.CostEstimate(flops=1_400_000_000, bytes_accessed=3_200_000, transcendentals=0),
        name="edge_sums",
    )(*args)


def main_sums(*args):
    return pl.pallas_call(
        main_kernel,
        out_shape=jax.ShapeDtypeStruct((32, 1, 1152), jnp.float32),
        in_specs=[SMEM, ANY, ANY, VMEM, VMEM],
        out_specs=VMEM,
        scratch_shapes=scratch(ROWS, SPAN, ROWS // 2) + [pltpu.SemaphoreType.DMA((6,))],
        compiler_params=pltpu.CompilerParams(vmem_limit_bytes=24 * 2**20),
        cost_estimate=pl.CostEstimate(flops=5_500_000_000, bytes_accessed=5_000_000, transcendentals=0),
        name="main_sums",
    )(*args)


def finish_kernel(parts, out):
    total = jnp.sum(parts[...], axis=0)
    scale = math.sqrt(L * CH)
    rows = jnp.concatenate([total[:, 128 * r : 128 * r + 128] for r in range(8)], axis=0)
    last = total[:, 1024:1152]
    lane = lax.broadcasted_iota(jnp.int32, (K, 128), 1)
    row = lax.broadcasted_iota(jnp.int32, (K, 128), 0)
    te = jnp.sum(jnp.where(lane == 64 + row, last, 0.0), axis=1, keepdims=True)
    both = jnp.concatenate([rows[:, 0:64], rows[:, 64:128]], axis=0)
    out[...] = both * scale * lax.rsqrt(last[:, 0:64] + 1e-06) * lax.rsqrt(te)


def finish(parts):
    return pl.pallas_call(
        finish_kernel,
        out_shape=jax.ShapeDtypeStruct((K, 64), jnp.float32),
        in_specs=[VMEM],
        out_specs=VMEM,
        compiler_params=pltpu.CompilerParams(vmem_limit_bytes=4 * 2**20),
        name="finish",
    )(parts)


def local(waveform, templates):
    tm = lax.axis_size("tm")
    chan = lax.axis_size("chan")
    me = lax.axis_index("tm")
    half = lax.rem(me // 8, 2)
    turn = lax.rem(me, 8) == 0
    place = jnp.stack([lax.rem(me, 2), half, turn.astype(jnp.int32)])
    plane = [[2 * i + h for i in range(tm // 2)] for h in range(2)]
    partner = [(i, i ^ 8) for i in range(tm)]

    shard = templates.reshape(K * SUB, -1)
    other = lax.ppermute(shard, "tm", [(i, i ^ 1) for i in range(tm)])
    got = lax.ppermute(first_pack(place, waveform), "tm", partner)

    def exchange(copies):
        return lax.all_to_all(copies, "tm", 0, 0, axis_index_groups=plane)

    own = exchange(lag_pack(shard))
    low, high = heads(waveform)
    low = lax.ppermute(low, "tm", [(16, 0)])
    high = lax.ppermute(high, "tm", [(16, 8)])
    other, got = lax.optimization_barrier((other, got))
    oth = exchange(lag_pack(other, 100_000_000_000))

    edges = edge_sums(place, waveform, got, low + high, own, oth)
    edges = lax.ppermute(edges, "tm", [(i, i - 1 if i % 8 else i + 7) for i in range(tm)])

    parts = main_sums(place, waveform, got, own, oth)
    edges = jnp.pad(edges.reshape(2, 4, 1, 1152), ((0, 0), (12, 0), (0, 0), (0, 0)))
    parts = parts + edges.reshape(parts.shape)
    pairs = [[t * chan + c for t in (i, i ^ 8) for c in range(chan)] for i in range(tm) if i & 8 == 0]
    parts = lax.all_to_all(parts, ("tm", "chan"), 0, 0, axis_index_groups=pairs)
    return finish(parts)


def solution(mesh):
    in_specs = (P("tm", "chan"), P(None, "tm", "chan"))
    out_specs = P(None, ("tm", "chan"))
    return jax.shard_map(local, mesh=mesh, in_specs=in_specs, out_specs=out_specs, check_vma=False)
```

```python
import math

import jax
import jax.numpy as jnp
from jax import lax
from jax.experimental import pallas as pl
from jax.experimental.pallas import tpu as pltpu
from jax.sharding import PartitionSpec as P

CH = 10240
L = 256
K = 16
SUB = 8
ROWS = 1024
RIM = 256
USED = ROWS + 16
SPAN = ROWS + 128
EDGE_USED = RIM + 16
EDGE_SPAN = RIM + 128
NN = (((1,), (0,)), ((), ()))
BF16 = jnp.bfloat16
VMEM = pl.BlockSpec(memory_space=pltpu.VMEM)
SMEM = pl.BlockSpec(memory_space=pltpu.SMEM)
ANY = pl.BlockSpec(memory_space=pl.ANY)


def swap(v):
    return jnp.concatenate([v[:, 64:], v[:, :64]], axis=1)


def low_lanes():
    return lax.broadcasted_iota(jnp.int32, (1, 128), 1) < 64


def pack_rest(v, half):
    n = v.shape[0] // 2
    if half == 0:
        return jnp.where(low_lanes(), v[:n], swap(v[n:]))
    return jnp.where(low_lanes(), swap(v[:n]), v[n:])


def first_pack_kernel(place, x, send, rest, sems):
    other = 1 - place[1]
    moves = [
        pltpu.make_async_copy(x.at[:, pl.ds(512, 128)], rest, sems.at[0]),
        pltpu.make_async_copy(x.at[:, lanes_of(other, 0)], send.at[pl.ds(0, ROWS)], sems.at[1]),
        pltpu.make_async_copy(x.at[:, lanes_of(other, 1)], send.at[pl.ds(ROWS, ROWS)], sems.at[2]),
    ]
    for move in moves:
        move.start()
    moves[0].wait()
    v = rest[...]
    send[2 * ROWS :] = jnp.where(other == 1, pack_rest(v, 1), pack_rest(v, 0))
    for move in moves[1:]:
        move.wait()


def lag_pack_kernel(lags, copies):
    i = lax.broadcasted_iota(jnp.int32, (K * SUB, K * SUB), 0)
    j = lax.broadcasted_iota(jnp.int32, (K * SUB, K * SUB), 1)
    order = (i // SUB * SUB + (SUB - 1 - i % SUB) == j).astype(BF16)
    v = lax.dot_general(order, lags[...], NN, preferred_element_type=jnp.float32).astype(BF16)
    for half in range(2):
        first, second = v[:, 256 * half : 256 * half + 128], v[:, 256 * half + 128 : 256 * half + 256]
        rest = pack_rest(v[:, 512:640], half)
        for p in range(16):
            if p // 4 % 2 == half:
                copies[p, 0:128] = first
                copies[p, 128:256] = second
                copies[p, 256:320] = rest


def first_pack(place, x):
    return pl.pallas_call(
        first_pack_kernel,
        out_shape=jax.ShapeDtypeStruct((ROWS * 5 // 2, 128), BF16),
        in_specs=[SMEM, ANY],
        out_specs=VMEM,
        scratch_shapes=[pltpu.VMEM((ROWS, 128), BF16), pltpu.SemaphoreType.DMA((3,))],
        compiler_params=pltpu.CompilerParams(vmem_limit_bytes=4 * 2**20),
        cost_estimate=pl.CostEstimate(flops=2_000_000, bytes_accessed=2_000_000, transcendentals=0),
        name="first_pack",
    )(place, x)


def lag_pack(lags, flops=2_000_000):
    return pl.pallas_call(
        lag_pack_kernel,
        out_shape=jax.ShapeDtypeStruct((16, 320, 128), BF16),
        in_specs=[VMEM],
        out_specs=VMEM,
        compiler_params=pltpu.CompilerParams(vmem_limit_bytes=4 * 2**20),
        cost_estimate=pl.CostEstimate(flops=flops, bytes_accessed=1_500_000, transcendentals=0),
        name="lag_pack",
    )(lags)


def pack_half(v, upper):
    return [
        jnp.where(upper, v[:, 256:384], v[:, 0:128]),
        jnp.where(upper, v[:, 384:512], v[:, 128:256]),
        jnp.where(upper, pack_rest(v[:, 512:640], 1), pack_rest(v[:, 512:640], 0)),
    ]


def both_heads(place, x, got):
    rest = got[2 * ROWS : 2 * ROWS + RIM]
    theirs = [
        got[0:RIM],
        got[ROWS : ROWS + RIM],
        jnp.where(low_lanes(), rest[0 : RIM // 2], swap(rest[RIM // 2 :])),
    ]
    upper = place[1] == 1
    mine = pack_half(x, upper)
    even = [jnp.where(upper, b, a) for a, b in zip(mine, theirs)]
    odd = [jnp.where(upper, a, b) for a, b in zip(mine, theirs)]
    return even, odd


def lanes_of(half, c):
    return pl.ds(pl.multiple_of(256 * half + 128 * c, 128), 128)


def lag_pair(ref, even, odd):
    pe, po = ref[even, 256:320], ref[odd, 256:320]
    rest = jnp.concatenate(
        [jnp.where(low_lanes(), pe, swap(po)), jnp.where(low_lanes(), swap(pe), po)], axis=0
    )
    return jnp.concatenate(
        [ref[even, 0:128], ref[even, 128:256], ref[odd, 0:128], ref[odd, 128:256], rest], axis=1
    )


def sum_lags(xm, x2, q, own, oth, used, with_energy):
    te = jnp.zeros((2 * K * SUB, 128), jnp.float32)
    for s in range(2):
        ws = []
        for a in range(4 * s, 4 * s + 4):
            w = jnp.concatenate([lag_pair(ref, 2 * a, 2 * a + 1) for ref in (own, oth)], axis=0)
            if with_energy:
                wf = w.astype(jnp.float32)
                sq = wf * wf
                for j in range(5):
                    te = te + sq[:, 128 * j : 128 * j + 128]
            for j in range(5):
                ws.append(jnp.transpose(w[:, 128 * j : 128 * j + 128]))
        w = jnp.concatenate(ws, axis=0)
        for b in range(2):
            rows = []
            for a in range(4 * s, 4 * s + 4):
                r = 32 * a
                rows += [xm[b, r : r + used], xm[b, r + 16 : r + 16 + used], x2[b, r : r + used]]
            part = lax.dot_general(jnp.concatenate(rows, axis=1), w, NN, preferred_element_type=jnp.float32)
            q[b, 0:used, :] = part if s == 0 else q[b, 0:used, :] + part
    te = jnp.sum(te.reshape(2, K, SUB, 128), axis=(0, 2))
    te = jnp.sum(te, axis=1, keepdims=True)
    lane = lax.broadcasted_iota(jnp.int32, (K, 128), 1)
    row = lax.broadcasted_iota(jnp.int32, (K, 128), 0)
    return jnp.sum(jnp.where(lane == 64 + row, te, 0.0), axis=0, keepdims=True)


def edge_lags(xm, x2, q, own, oth):
    parts = []
    for s, first in ((0, 144), (1, 16)):
        n = EDGE_USED - first
        ws, rows = [], []
        for a in range(4 * s, 4 * s + 4):
            ws.append(jnp.concatenate([lag_pair(ref, 2 * a, 2 * a + 1) for ref in (own, oth)], axis=0))
            r = 32 * a + first
            two = lambda ref, r: jnp.concatenate([ref[b, r : r + n] for b in range(2)], axis=0)
            rows += [two(xm, r), two(xm, r + 16), two(x2, r)]
        parts.append(
            lax.dot_general(
                jnp.concatenate(rows, axis=1),
                jnp.concatenate(ws, axis=1),
                (((1,), (1,)), ((), ())),
                preferred_element_type=jnp.float32,
            )
        )
    for b in range(2):
        q[b, 0:16, :] = jnp.zeros((16, 2 * K * SUB), jnp.float32)
        q[b, 16:144, :] = parts[1][256 * b : 256 * b + 128]
        q[b, 144:EDGE_USED, :] = parts[1][256 * b + 128 : 256 * b + 256] + parts[0][128 * b : 128 * b + 128]


def sum_fine_lags(q, b, span, used, z):
    q[b, used:span, :] = jnp.zeros((span - used, 2 * K * SUB), jnp.float32)
    sums = []
    for g in range(2):
        p = jnp.transpose(q[b, :, 128 * g : 128 * g + 128])
        p = p.reshape(K, SUB, span)
        p = pltpu.roll(p, span - (SUB - 1), 2, stride=1, stride_axis=1)
        sums.append(jnp.sum(p, axis=1))
    late = [pltpu.roll(p, span - SUB, 1) for p in sums]
    return jnp.where(z == 1, late[0] + sums[1], sums[0] + late[1])


def window_energy(xm, x2, b, n):
    sq = jnp.zeros((n, 128), jnp.float32)
    rest = x2[b, 0:n]
    for v in (xm[b, 0:n, 0:128], xm[b, 0:n, 128:256], jnp.where(low_lanes(), rest, jnp.zeros_like(rest))):
        v = v.astype(jnp.float32)
        sq = sq + v * v
    de = jnp.sum(jnp.transpose(sq), axis=0, keepdims=True)
    de = jnp.broadcast_to(de, (8, n))
    for i in range(8):
        de = de + pltpu.roll(de, n - (1 << i), 1)
    return de


def store(out, at, stack, de, te_row, count):
    low = low_lanes()
    for d in range(count):
        tile = slice(128 * (d // 2), 128 * (d // 2) + 128)
        lo, hi, en = stack[0:8, tile], stack[8:16, tile], de[:, tile]
        if d % 2 == 0:
            hi = pltpu.roll(hi, 64, 1)
        else:
            lo, en = pltpu.roll(lo, 64, 1), pltpu.roll(en, 64, 1)
        both = jnp.where(low, lo, hi)
        for r in range(8):
            out[at + d, :, 128 * r : 128 * r + 128] = both[r : r + 1]
        out[at + d, :, 1024:1152] = jnp.where(low, en[0:1], te_row)


def lay_out_rest(x2, b, left, right, before, after):
    zeros = [jnp.zeros((n, 128), BF16) for n in (before, after)]
    left = jnp.concatenate([v for v in (zeros[0], left, zeros[1]) if v.shape[0]], axis=0)
    right = jnp.concatenate([v for v in (zeros[0], right, zeros[1]) if v.shape[0]], axis=0)
    n = left.shape[0]
    x2[b, 0 : n - 16] = jnp.where(low_lanes(), left[0 : n - 16], right[16:n])
    x2[b, n - 16 : n] = jnp.where(low_lanes(), left[n - 16 : n], jnp.zeros((16, 128), BF16))


def fetch(x, got, half, rows, at, xm, mine, his, sems):
    first = [
        pltpu.make_async_copy(x.at[pl.ds(0, rows), pl.ds(512, 128)], mine, sems.at[0]),
        pltpu.make_async_copy(got.at[pl.ds(2 * ROWS, his.shape[0])], his, sems.at[1]),
    ]
    second = []
    for c in range(2):
        lanes, body = pl.ds(128 * c, 128), pl.ds(at, rows)
        second += [
            pltpu.make_async_copy(x.at[pl.ds(0, rows), lanes_of(half, c)], xm.at[0, body, lanes], sems.at[2 + c]),
            pltpu.make_async_copy(got.at[pl.ds(ROWS * c, rows)], xm.at[1, body, lanes], sems.at[4 + c]),
        ]
    for move in first + second:
        move.start()
    return first, second


def edge_kernel(place, x, got, third, own, oth, edges, xm, x2, q, rows, sem):
    move = pltpu.make_async_copy(x.at[pl.ds(0, RIM)], rows, sem.at[0])
    move.start()
    for b in range(2):
        xm[b, 0:RIM] = jnp.zeros((RIM, 256), BF16)
    move.wait()
    even, odd = both_heads(place, rows[...], got)
    turn = place[2] == 1
    after = [third[0:RIM], third[RIM : 2 * RIM], third[2 * RIM :]]
    heads = [
        [jnp.where(turn, n, v) for v, n in zip(even, odd)],
        [jnp.where(turn, n, v) for v, n in zip(odd, after)],
    ]
    for b in range(2):
        for c in range(2):
            xm[b, RIM:, 128 * c : 128 * c + 128] = heads[b][c]
        p = heads[b][2]
        left, right = jnp.concatenate([p, swap(p)], axis=0), jnp.concatenate([swap(p), p], axis=0)
        lay_out_rest(x2, b, left, right, RIM, 0)
    edge_lags(xm, x2, q, own, oth)
    for b in range(2):
        stack = sum_fine_lags(q, b, EDGE_SPAN, EDGE_USED, place[0])
        de = window_energy(xm, x2, b, 2 * RIM)
        store(edges, 4 * b, stack, de, jnp.zeros((1, 128), jnp.float32), 4)


def layout_kernel(place, x, got, low, high, xm, x2, energy, mine, his, rows, sems):
    half = place[1]
    head = pltpu.make_async_copy(x.at[pl.ds(0, RIM)], rows, sems.at[6])
    head.start()
    first, second = fetch(x, got, half, ROWS, 0, xm, mine, his, sems)
    for move in first:
        move.wait()
    for b in range(2):
        xm[b, ROWS:] = jnp.zeros((RIM, 256), BF16)
        if b == 0:
            v = mine[...]
            left, right = jnp.where(half == 1, swap(v), v), jnp.where(half == 1, v, swap(v))
        else:
            p = his[...]
            left, right = jnp.concatenate([p, swap(p)], axis=0), jnp.concatenate([swap(p), p], axis=0)
        lay_out_rest(x2, b, left, right, 0, RIM)
    head.wait()
    v = rows[...]
    for h, out in enumerate((low, high)):
        out[0:RIM] = v[:, 256 * h : 256 * h + 128]
        out[RIM : 2 * RIM] = v[:, 256 * h + 128 : 256 * h + 256]
        out[2 * RIM :] = pack_rest(v[:, 512:640], h)
    for move in second:
        move.wait()
    for b in range(2):
        energy[b] = window_energy(xm, x2, b, ROWS + RIM)


def main_kernel(place, xm, x2, energy, own, oth, out, q):
    te_row = sum_lags(xm, x2, q, own, oth, USED, True)
    for b in range(2):
        stack = sum_fine_lags(q, b, SPAN, USED, place[0])
        store(out, 16 * jnp.where(place[1] == b, 0, 1), stack, energy[b], te_row, 16)


def edge_sums(*args):
    return pl.pallas_call(
        edge_kernel,
        out_shape=jax.ShapeDtypeStruct((8, 1, 1152), jnp.float32),
        in_specs=[SMEM, ANY, VMEM, VMEM, VMEM, VMEM],
        out_specs=VMEM,
        scratch_shapes=[
            pltpu.VMEM((2, 2 * RIM, 256), BF16),
            pltpu.VMEM((2, 2 * RIM, 128), BF16),
            pltpu.VMEM((2, EDGE_SPAN, 2 * K * SUB), jnp.float32),
            pltpu.VMEM((RIM, 640), BF16),
            pltpu.SemaphoreType.DMA((1,)),
        ],
        compiler_params=pltpu.CompilerParams(vmem_limit_bytes=10 * 2**20),
        cost_estimate=pl.CostEstimate(flops=1_400_000_000, bytes_accessed=3_200_000, transcendentals=0),
        name="edge_sums",
    )(*args)


def layout(place, x, got):
    n = ROWS + RIM
    one = jax.ShapeDtypeStruct((RIM * 5 // 2, 128), BF16)
    return pl.pallas_call(
        layout_kernel,
        out_shape=(
            one,
            one,
            jax.ShapeDtypeStruct((2, n, 256), BF16),
            jax.ShapeDtypeStruct((2, n, 128), BF16),
            jax.ShapeDtypeStruct((2, 8, n), jnp.float32),
        ),
        in_specs=[SMEM, ANY, ANY],
        out_specs=(VMEM,) * 5,
        scratch_shapes=[
            pltpu.VMEM((ROWS, 128), BF16),
            pltpu.VMEM((ROWS // 2, 128), BF16),
            pltpu.VMEM((RIM, 640), BF16),
            pltpu.SemaphoreType.DMA((7,)),
        ],
        compiler_params=pltpu.CompilerParams(vmem_limit_bytes=12 * 2**20),
        cost_estimate=pl.CostEstimate(flops=4_000_000, bytes_accessed=4_500_000, transcendentals=0),
        name="layout",
    )(place, x, got)


def main_sums(*args):
    return pl.pallas_call(
        main_kernel,
        out_shape=jax.ShapeDtypeStruct((32, 1, 1152), jnp.float32),
        in_specs=[SMEM] + [VMEM] * 5,
        out_specs=VMEM,
        scratch_shapes=[pltpu.VMEM((2, SPAN, 2 * K * SUB), jnp.float32)],
        compiler_params=pltpu.CompilerParams(vmem_limit_bytes=24 * 2**20),
        cost_estimate=pl.CostEstimate(flops=5_500_000_000, bytes_accessed=5_000_000, transcendentals=0),
        name="main_sums",
    )(*args)


def finish_kernel(parts, out):
    total = jnp.sum(parts[...], axis=0)
    scale = math.sqrt(L * CH)
    rows = jnp.concatenate([total[:, 128 * r : 128 * r + 128] for r in range(8)], axis=0)
    last = total[:, 1024:1152]
    lane = lax.broadcasted_iota(jnp.int32, (K, 128), 1)
    row = lax.broadcasted_iota(jnp.int32, (K, 128), 0)
    te = jnp.sum(jnp.where(lane == 64 + row, last, 0.0), axis=1, keepdims=True)
    both = jnp.concatenate([rows[:, 0:64], rows[:, 64:128]], axis=0)
    out[...] = both * scale * lax.rsqrt(last[:, 0:64] + 1e-06) * lax.rsqrt(te)


def finish(parts):
    return pl.pallas_call(
        finish_kernel,
        out_shape=jax.ShapeDtypeStruct((K, 64), jnp.float32),
        in_specs=[VMEM],
        out_specs=VMEM,
        compiler_params=pltpu.CompilerParams(vmem_limit_bytes=4 * 2**20),
        name="finish",
    )(parts)


def local(waveform, templates):
    tm = lax.axis_size("tm")
    chan = lax.axis_size("chan")
    me = lax.axis_index("tm")
    half = lax.rem(me // 8, 2)
    turn = lax.rem(me, 8) == 0
    place = jnp.stack([lax.rem(me, 2), half, turn.astype(jnp.int32)])
    plane = [[2 * i + h for i in range(tm // 2)] for h in range(2)]
    partner = [(i, i ^ 8) for i in range(tm)]

    shard = templates.reshape(K * SUB, -1)
    other = lax.ppermute(shard, "tm", [(i, i ^ 1) for i in range(tm)])
    got = lax.ppermute(first_pack(place, waveform), "tm", partner)

    def exchange(copies):
        return lax.all_to_all(copies, "tm", 0, 0, axis_index_groups=plane)

    own = exchange(lag_pack(shard))
    other, got = lax.optimization_barrier((other, got))
    low, high, *rows = layout(place, waveform, got)
    low = lax.ppermute(low, "tm", [(16, 0)])
    high = lax.ppermute(high, "tm", [(16, 8)])
    oth = exchange(lag_pack(other, 100_000_000_000))

    edges = edge_sums(place, waveform, got, low + high, own, oth)
    edges = lax.ppermute(edges, "tm", [(i, i - 1 if i % 8 else i + 7) for i in range(tm)])

    parts = main_sums(place, *rows, own, oth)
    edges = jnp.pad(edges.reshape(2, 4, 1, 1152), ((0, 0), (12, 0), (0, 0), (0, 0)))
    parts = parts + edges.reshape(parts.shape)
    pairs = [[t * chan + c for t in (i, i ^ 8) for c in range(chan)] for i in range(tm) if i & 8 == 0]
    parts = lax.all_to_all(parts, ("tm", "chan"), 0, 0, axis_index_groups=pairs)
    return finish(parts)


def solution(mesh):
    in_specs = (P("tm", "chan"), P(None, "tm", "chan"))
    out_specs = P(None, ("tm", "chan"))
    return jax.shard_map(local, mesh=mesh, in_specs=in_specs, out_specs=out_specs, check_vma=False)
```

```python
import math

import jax
import jax.numpy as jnp
from jax import lax
from jax.experimental import pallas as pl
from jax.experimental.pallas import tpu as pltpu
from jax.sharding import PartitionSpec as P

CH = 10240
L = 256
K = 16
SUB = 8
ROWS = 1024
RIM = 256
USED = ROWS + 16
SPAN = ROWS + 128
EDGE_USED = RIM + 16
EDGE_SPAN = RIM + 128
NN = (((1,), (0,)), ((), ()))
BF16 = jnp.bfloat16
VMEM = pl.BlockSpec(memory_space=pltpu.VMEM)
SMEM = pl.BlockSpec(memory_space=pltpu.SMEM)
ANY = pl.BlockSpec(memory_space=pl.ANY)


def swap(v):
    return jnp.concatenate([v[:, 64:], v[:, :64]], axis=1)


def low_lanes():
    return lax.broadcasted_iota(jnp.int32, (1, 128), 1) < 64


def pack_rest(v, half):
    n = v.shape[0] // 2
    if half == 0:
        return jnp.where(low_lanes(), v[:n], swap(v[n:]))
    return jnp.where(low_lanes(), swap(v[:n]), v[n:])


def first_pack_kernel(place, x, send, rest, sems):
    other = 1 - place[1]
    moves = [
        pltpu.make_async_copy(x.at[:, pl.ds(512, 128)], rest, sems.at[0]),
        pltpu.make_async_copy(x.at[:, lanes_of(other, 0)], send.at[pl.ds(0, ROWS)], sems.at[1]),
        pltpu.make_async_copy(x.at[:, lanes_of(other, 1)], send.at[pl.ds(ROWS, ROWS)], sems.at[2]),
    ]
    for move in moves:
        move.start()
    moves[0].wait()
    v = rest[...]
    send[2 * ROWS :] = jnp.where(other == 1, pack_rest(v, 1), pack_rest(v, 0))
    for move in moves[1:]:
        move.wait()


def lag_pack_kernel(lags, copies):
    i = lax.broadcasted_iota(jnp.int32, (K * SUB, K * SUB), 0)
    j = lax.broadcasted_iota(jnp.int32, (K * SUB, K * SUB), 1)
    order = (i // SUB * SUB + (SUB - 1 - i % SUB) == j).astype(BF16)
    v = lax.dot_general(order, lags[...], NN, preferred_element_type=jnp.float32).astype(BF16)
    for half in range(2):
        first, second = v[:, 256 * half : 256 * half + 128], v[:, 256 * half + 128 : 256 * half + 256]
        rest = pack_rest(v[:, 512:640], half)
        for p in range(16):
            if p // 4 % 2 == half:
                copies[p, 0:128] = first
                copies[p, 128:256] = second
                copies[p, 256:320] = rest


def first_pack(place, x):
    return pl.pallas_call(
        first_pack_kernel,
        out_shape=jax.ShapeDtypeStruct((ROWS * 5 // 2, 128), BF16),
        in_specs=[SMEM, ANY],
        out_specs=VMEM,
        scratch_shapes=[pltpu.VMEM((ROWS, 128), BF16), pltpu.SemaphoreType.DMA((3,))],
        compiler_params=pltpu.CompilerParams(vmem_limit_bytes=4 * 2**20),
        cost_estimate=pl.CostEstimate(flops=2_000_000, bytes_accessed=2_000_000, transcendentals=0),
        name="first_pack",
    )(place, x)


def lag_pack(lags, flops=2_000_000):
    return pl.pallas_call(
        lag_pack_kernel,
        out_shape=jax.ShapeDtypeStruct((16, 320, 128), BF16),
        in_specs=[VMEM],
        out_specs=VMEM,
        compiler_params=pltpu.CompilerParams(vmem_limit_bytes=4 * 2**20),
        cost_estimate=pl.CostEstimate(flops=flops, bytes_accessed=1_500_000, transcendentals=0),
        name="lag_pack",
    )(lags)


def pack_half(v, upper):
    return [
        jnp.where(upper, v[:, 256:384], v[:, 0:128]),
        jnp.where(upper, v[:, 384:512], v[:, 128:256]),
        jnp.where(upper, pack_rest(v[:, 512:640], 1), pack_rest(v[:, 512:640], 0)),
    ]


def both_heads(place, x, got):
    rest = got[2 * ROWS : 2 * ROWS + RIM]
    theirs = [
        got[0:RIM],
        got[ROWS : ROWS + RIM],
        jnp.where(low_lanes(), rest[0 : RIM // 2], swap(rest[RIM // 2 :])),
    ]
    upper = place[1] == 1
    mine = pack_half(x, upper)
    even = [jnp.where(upper, b, a) for a, b in zip(mine, theirs)]
    odd = [jnp.where(upper, a, b) for a, b in zip(mine, theirs)]
    return even, odd


def lanes_of(half, c):
    return pl.ds(pl.multiple_of(256 * half + 128 * c, 128), 128)


def lag_pair(ref, even, odd):
    pe, po = ref[even, 256:320], ref[odd, 256:320]
    rest = jnp.concatenate(
        [jnp.where(low_lanes(), pe, swap(po)), jnp.where(low_lanes(), swap(pe), po)], axis=0
    )
    return jnp.concatenate(
        [ref[even, 0:128], ref[even, 128:256], ref[odd, 0:128], ref[odd, 128:256], rest], axis=1
    )


def sum_lags(xm, x2, q, own, oth, used, with_energy):
    te = jnp.zeros((2 * K * SUB, 128), jnp.float32)
    for s in range(2):
        ws = []
        for a in range(4 * s, 4 * s + 4):
            w = jnp.concatenate([lag_pair(ref, 2 * a, 2 * a + 1) for ref in (own, oth)], axis=0)
            if with_energy:
                wf = w.astype(jnp.float32)
                sq = wf * wf
                for j in range(5):
                    te = te + sq[:, 128 * j : 128 * j + 128]
            for j in range(5):
                ws.append(jnp.transpose(w[:, 128 * j : 128 * j + 128]))
        w = jnp.concatenate(ws, axis=0)
        for b in range(2):
            rows = []
            for a in range(4 * s, 4 * s + 4):
                r = 32 * a
                rows += [xm[b, r : r + used], xm[b, r + 16 : r + 16 + used], x2[b, r : r + used]]
            part = lax.dot_general(jnp.concatenate(rows, axis=1), w, NN, preferred_element_type=jnp.float32)
            q[b, 0:used, :] = part if s == 0 else q[b, 0:used, :] + part
    te = jnp.sum(te.reshape(2, K, SUB, 128), axis=(0, 2))
    te = jnp.sum(te, axis=1, keepdims=True)
    lane = lax.broadcasted_iota(jnp.int32, (K, 128), 1)
    row = lax.broadcasted_iota(jnp.int32, (K, 128), 0)
    return jnp.sum(jnp.where(lane == 64 + row, te, 0.0), axis=0, keepdims=True)


def edge_lags(xm, x2, q, own, oth):
    parts = []
    for s, first in ((0, 144), (1, 16)):
        n = EDGE_USED - first
        ws, rows = [], []
        for a in range(4 * s, 4 * s + 4):
            ws.append(jnp.concatenate([lag_pair(ref, 2 * a, 2 * a + 1) for ref in (own, oth)], axis=0))
            r = 32 * a + first
            two = lambda ref, r: jnp.concatenate([ref[b, r : r + n] for b in range(2)], axis=0)
            rows += [two(xm, r), two(xm, r + 16), two(x2, r)]
        parts.append(
            lax.dot_general(
                jnp.concatenate(rows, axis=1),
                jnp.concatenate(ws, axis=1),
                (((1,), (1,)), ((), ())),
                preferred_element_type=jnp.float32,
            )
        )
    for b in range(2):
        q[b, 0:16, :] = jnp.zeros((16, 2 * K * SUB), jnp.float32)
        q[b, 16:144, :] = parts[1][256 * b : 256 * b + 128]
        q[b, 144:EDGE_USED, :] = parts[1][256 * b + 128 : 256 * b + 256] + parts[0][128 * b : 128 * b + 128]


def sum_fine_lags(q, b, span, used, z):
    q[b, used:span, :] = jnp.zeros((span - used, 2 * K * SUB), jnp.float32)
    sums = []
    for g in range(2):
        p = jnp.transpose(q[b, :, 128 * g : 128 * g + 128])
        p = p.reshape(K, SUB, span)
        p = pltpu.roll(p, span - (SUB - 1), 2, stride=1, stride_axis=1)
        sums.append(jnp.sum(p, axis=1))
    late = [pltpu.roll(p, span - SUB, 1) for p in sums]
    return jnp.where(z == 1, late[0] + sums[1], sums[0] + late[1])


def window_energy(xm, x2, b, n):
    sq = jnp.zeros((n, 128), jnp.float32)
    rest = x2[b, 0:n]
    for v in (xm[b, 0:n, 0:128], xm[b, 0:n, 128:256], jnp.where(low_lanes(), rest, jnp.zeros_like(rest))):
        v = v.astype(jnp.float32)
        sq = sq + v * v
    de = jnp.sum(jnp.transpose(sq), axis=0, keepdims=True)
    de = jnp.broadcast_to(de, (8, n))
    for i in range(8):
        de = de + pltpu.roll(de, n - (1 << i), 1)
    return de


def store(out, at, stack, de, te_row, count):
    low = low_lanes()
    for d in range(count):
        tile = slice(128 * (d // 2), 128 * (d // 2) + 128)
        lo, hi, en = stack[0:8, tile], stack[8:16, tile], de[:, tile]
        if d % 2 == 0:
            hi = pltpu.roll(hi, 64, 1)
        else:
            lo, en = pltpu.roll(lo, 64, 1), pltpu.roll(en, 64, 1)
        both = jnp.where(low, lo, hi)
        for r in range(8):
            out[at + d, :, 128 * r : 128 * r + 128] = both[r : r + 1]
        out[at + d, :, 1024:1152] = jnp.where(low, en[0:1], te_row)


def lay_out_rest(x2, b, left, right, before, after):
    zeros = [jnp.zeros((n, 128), BF16) for n in (before, after)]
    left = jnp.concatenate([v for v in (zeros[0], left, zeros[1]) if v.shape[0]], axis=0)
    right = jnp.concatenate([v for v in (zeros[0], right, zeros[1]) if v.shape[0]], axis=0)
    n = left.shape[0]
    x2[b, 0 : n - 16] = jnp.where(low_lanes(), left[0 : n - 16], right[16:n])
    x2[b, n - 16 : n] = jnp.where(low_lanes(), left[n - 16 : n], jnp.zeros((16, 128), BF16))


def fetch(x, got, half, rows, at, xm, mine, his, sems):
    first = [
        pltpu.make_async_copy(x.at[pl.ds(0, rows), pl.ds(512, 128)], mine, sems.at[0]),
        pltpu.make_async_copy(got.at[pl.ds(2 * ROWS, his.shape[0])], his, sems.at[1]),
    ]
    second = []
    for c in range(2):
        lanes, body = pl.ds(128 * c, 128), pl.ds(at, rows)
        second += [
            pltpu.make_async_copy(x.at[pl.ds(0, rows), lanes_of(half, c)], xm.at[0, body, lanes], sems.at[2 + c]),
            pltpu.make_async_copy(got.at[pl.ds(ROWS * c, rows)], xm.at[1, body, lanes], sems.at[4 + c]),
        ]
    for move in first + second:
        move.start()
    return first, second


def edge_kernel(place, x, got, third, own, oth, edges, xm, x2, q, rows, sem):
    move = pltpu.make_async_copy(x.at[pl.ds(0, RIM)], rows, sem.at[0])
    move.start()
    for b in range(2):
        xm[b, 0:RIM] = jnp.zeros((RIM, 256), BF16)
    move.wait()
    even, odd = both_heads(place, rows[...], got)
    turn = place[2] == 1
    after = [third[0:RIM], third[RIM : 2 * RIM], third[2 * RIM :]]
    heads = [
        [jnp.where(turn, n, v) for v, n in zip(even, odd)],
        [jnp.where(turn, n, v) for v, n in zip(odd, after)],
    ]
    for b in range(2):
        for c in range(2):
            xm[b, RIM:, 128 * c : 128 * c + 128] = heads[b][c]
        p = heads[b][2]
        left, right = jnp.concatenate([p, swap(p)], axis=0), jnp.concatenate([swap(p), p], axis=0)
        lay_out_rest(x2, b, left, right, RIM, 0)
    edge_lags(xm, x2, q, own, oth)
    for b in range(2):
        stack = sum_fine_lags(q, b, EDGE_SPAN, EDGE_USED, place[0])
        de = window_energy(xm, x2, b, 2 * RIM)
        store(edges, 4 * b, stack, de, jnp.zeros((1, 128), jnp.float32), 4)


def layout_kernel(place, x, got, low, high, xm, x2, energy, mine, his, rows, sems):
    half = place[1]
    head = pltpu.make_async_copy(x.at[pl.ds(0, RIM)], rows, sems.at[6])
    head.start()
    first, second = fetch(x, got, half, ROWS, 0, xm, mine, his, sems)
    for move in first:
        move.wait()
    for b in range(2):
        xm[b, ROWS:] = jnp.zeros((RIM, 256), BF16)
        if b == 0:
            v = mine[...]
            left, right = jnp.where(half == 1, swap(v), v), jnp.where(half == 1, v, swap(v))
        else:
            p = his[...]
            left, right = jnp.concatenate([p, swap(p)], axis=0), jnp.concatenate([swap(p), p], axis=0)
        lay_out_rest(x2, b, left, right, 0, RIM)
    head.wait()
    v = rows[...]
    for h, out in enumerate((low, high)):
        out[0:RIM] = v[:, 256 * h : 256 * h + 128]
        out[RIM : 2 * RIM] = v[:, 256 * h + 128 : 256 * h + 256]
        out[2 * RIM :] = pack_rest(v[:, 512:640], h)
    for move in second:
        move.wait()
    for b in range(2):
        energy[b] = window_energy(xm, x2, b, ROWS + RIM)


def main_kernel(place, xm, x2, energy, own, oth, out, q):
    te_row = sum_lags(xm, x2, q, own, oth, USED, True)
    for b in range(2):
        stack = sum_fine_lags(q, b, SPAN, USED, place[0])
        store(out, 16 * jnp.where(place[1] == b, 0, 1), stack, energy[b], te_row, 16)


def edge_sums(*args):
    return pl.pallas_call(
        edge_kernel,
        out_shape=jax.ShapeDtypeStruct((8, 1, 1152), jnp.float32),
        in_specs=[SMEM, ANY, VMEM, VMEM, VMEM, VMEM],
        out_specs=VMEM,
        scratch_shapes=[
            pltpu.VMEM((2, 2 * RIM, 256), BF16),
            pltpu.VMEM((2, 2 * RIM, 128), BF16),
            pltpu.VMEM((2, EDGE_SPAN, 2 * K * SUB), jnp.float32),
            pltpu.VMEM((RIM, 640), BF16),
            pltpu.SemaphoreType.DMA((1,)),
        ],
        compiler_params=pltpu.CompilerParams(vmem_limit_bytes=10 * 2**20),
        cost_estimate=pl.CostEstimate(flops=1_400_000_000, bytes_accessed=3_200_000, transcendentals=0),
        name="edge_sums",
    )(*args)


def layout(place, x, got):
    n = ROWS + RIM
    one = jax.ShapeDtypeStruct((RIM * 5 // 2, 128), BF16)
    return pl.pallas_call(
        layout_kernel,
        out_shape=(
            one,
            one,
            jax.ShapeDtypeStruct((2, n, 256), BF16),
            jax.ShapeDtypeStruct((2, n, 128), BF16),
            jax.ShapeDtypeStruct((2, 8, n), jnp.float32),
        ),
        in_specs=[SMEM, ANY, ANY],
        out_specs=(VMEM,) * 5,
        scratch_shapes=[
            pltpu.VMEM((ROWS, 128), BF16),
            pltpu.VMEM((ROWS // 2, 128), BF16),
            pltpu.VMEM((RIM, 640), BF16),
            pltpu.SemaphoreType.DMA((7,)),
        ],
        compiler_params=pltpu.CompilerParams(vmem_limit_bytes=12 * 2**20),
        cost_estimate=pl.CostEstimate(flops=3_000_000_000, bytes_accessed=4_500_000, transcendentals=0),
        name="layout",
    )(place, x, got)


def main_sums(*args):
    return pl.pallas_call(
        main_kernel,
        out_shape=jax.ShapeDtypeStruct((32, 1, 1152), jnp.float32),
        in_specs=[SMEM] + [VMEM] * 5,
        out_specs=VMEM,
        scratch_shapes=[pltpu.VMEM((2, SPAN, 2 * K * SUB), jnp.float32)],
        compiler_params=pltpu.CompilerParams(vmem_limit_bytes=24 * 2**20),
        cost_estimate=pl.CostEstimate(flops=5_500_000_000, bytes_accessed=5_000_000, transcendentals=0),
        name="main_sums",
    )(*args)


def finish_kernel(parts, out):
    total = jnp.sum(parts[...], axis=0)
    scale = math.sqrt(L * CH)
    rows = jnp.concatenate([total[:, 128 * r : 128 * r + 128] for r in range(8)], axis=0)
    last = total[:, 1024:1152]
    lane = lax.broadcasted_iota(jnp.int32, (K, 128), 1)
    row = lax.broadcasted_iota(jnp.int32, (K, 128), 0)
    te = jnp.sum(jnp.where(lane == 64 + row, last, 0.0), axis=1, keepdims=True)
    both = jnp.concatenate([rows[:, 0:64], rows[:, 64:128]], axis=0)
    out[...] = both * scale * lax.rsqrt(last[:, 0:64] + 1e-06) * lax.rsqrt(te)


def finish(parts):
    return pl.pallas_call(
        finish_kernel,
        out_shape=jax.ShapeDtypeStruct((K, 64), jnp.float32),
        in_specs=[VMEM],
        out_specs=VMEM,
        compiler_params=pltpu.CompilerParams(vmem_limit_bytes=4 * 2**20),
        name="finish",
    )(parts)


def local(waveform, templates):
    tm = lax.axis_size("tm")
    chan = lax.axis_size("chan")
    me = lax.axis_index("tm")
    half = lax.rem(me // 8, 2)
    turn = lax.rem(me, 8) == 0
    place = jnp.stack([lax.rem(me, 2), half, turn.astype(jnp.int32)])
    plane = [[2 * i + h for i in range(tm // 2)] for h in range(2)]
    partner = [(i, i ^ 8) for i in range(tm)]

    shard = templates.reshape(K * SUB, -1)
    other = lax.ppermute(shard, "tm", [(i, i ^ 1) for i in range(tm)])
    got = lax.ppermute(first_pack(place, waveform), "tm", partner)

    def exchange(copies):
        return lax.all_to_all(copies, "tm", 0, 0, axis_index_groups=plane)

    own = exchange(lag_pack(shard))
    other, got = lax.optimization_barrier((other, got))
    low, high, *rows = layout(place, waveform, got)
    low = lax.ppermute(low, "tm", [(16, 0)])
    high = lax.ppermute(high, "tm", [(16, 8)])
    oth = exchange(lag_pack(other, 100_000_000_000))

    edges = edge_sums(place, waveform, got, low + high, own, oth)
    edges = lax.ppermute(edges, "tm", [(i, i - 1 if i % 8 else i + 7) for i in range(tm)])

    parts = main_sums(place, *rows, own, oth)
    edges = jnp.pad(edges.reshape(2, 4, 1, 1152), ((0, 0), (12, 0), (0, 0), (0, 0)))
    parts = parts + edges.reshape(parts.shape)
    pairs = [[t * chan + c for t in (i, i ^ 8) for c in range(chan)] for i in range(tm) if i & 8 == 0]
    parts = lax.all_to_all(parts, ("tm", "chan"), 0, 0, axis_index_groups=pairs)
    return finish(parts)


def solution(mesh):
    in_specs = (P("tm", "chan"), P(None, "tm", "chan"))
    out_specs = P(None, ("tm", "chan"))
    return jax.shard_map(local, mesh=mesh, in_specs=in_specs, out_specs=out_specs, check_vma=False)
```
